256 devices in a mesh: row: 32 (over x, z), col: 8 (over y, core).
Axes of the slice: x: 4, y: 4, z: 8, core: 2. Of those that a mesh axis runs over, the one named last changes fastest.
Arguments:
- a_blocks: bfloat16 [32, 8, 64, 65536], P('row', 'col'), may hold values from -0.75 to 0.75
- a_rows: int32 [32, 8, 1024], P('row', 'col'), may hold values from 0 to 255
- a_steps: int32 [32, 8, 1024], P('row', 'col'), may hold values from 0 to 2
- a_cols: int32 [32, 8, 1024], P('row', 'col'), may hold values from 0 to 65
- a_live: int32 [32, 8], P('row', 'col'), may hold values from 256 to 1024, as said below
- p_blocks: bfloat16 [128, 512, 64, 128], P('row', 'col'), may hold values from -0.8984375 to 0.8984375
Outputs:
- coarse_op: float32 [4096, 9216], P('row', 'col')
The draws below stay inside these ranges and needn't reach their ends.
Inputs may be any that keep to these rules, and one draw needn't show every extreme that they name: `a_live`: blocks at or beyond a device's count are padding; one device in every draw holds 1024 live blocks.
All inputs are finite; a program needn't handle non-finite values.
Results may differ from the reference program's by a relative error of at most 0.0029.
Values may be sent and summed in bfloat16 or wider, within the bound.
No kernel may reach another device: no remote copies, remote signals or barrier semaphores. Data moves between devices by JAX's collectives and lax.ppermute only.
A program may use at most 192 MiB of HBM per device.

```python
import jax
import jax.numpy as jnp
from jax import lax

BLOCK = 64
SLOTS = 2
SX = 4
SY = 64
AGG_DEV = 2
CAPACITY = 1024
FINE_DEV = 256
NX = 128
NY = 512
N_ROW = 32
N_COL = 8


def draw_a_live(key, part):
    key_base, key_top = jax.random.split(jax.random.fold_in(key, 11))
    device_count = N_ROW * N_COL
    base_counts = jax.random.randint(key_base, (device_count,), CAPACITY // 4, CAPACITY // 2 + 1)
    top_device = jax.random.randint(key_top, (), 0, device_count)
    flat_counts = jnp.where(jnp.arange(device_count) == top_device, CAPACITY, base_counts)
    return flat_counts.reshape(N_ROW, N_COL).astype(jnp.int32)


def set_ends(array, own_key, low, high):
    extent = array.shape
    index_at = [jax.random.randint(jax.random.fold_in(own_key, axis), (), 0, extent[axis]) for axis in range(len(extent))]
    array = array.at[tuple(index_at)].set(low)
    longest = extent.index(max(extent))
    index_at[longest] = (index_at[longest] + 1) % extent[longest]
    return array.at[tuple(index_at)].set(high)


def steps_of(key, shape, pieces, smallest, top_value):
    factor_of, own = 1.0, jax.random.fold_in(key, 6)
    for axis_at, shards_of in pieces:
        heights = jnp.exp(jax.random.uniform(jax.random.fold_in(own, axis_at), (shards_of,), jnp.float32, smallest / len(pieces), top_value / len(pieces)))
        factor_of = factor_of * jnp.repeat(heights, shape[axis_at] // shards_of).reshape([-1 if axis == axis_at else 1 for axis in range(len(shape))])
    return factor_of


def gaussian(own_key, extent, width, limit, shards=(), kind=jnp.bfloat16):
    level = steps_of(own_key, extent, shards, -0.22, 0.18) if shards else 1.0
    entries = jax.random.normal(own_key, extent, jnp.float32) * width * level
    return jnp.minimum(jnp.maximum(entries, -limit), limit).astype(kind)


def setup_inputs(seed: int = 0) -> dict:
    arg_keys = jax.random.split(jax.random.key(seed), 7)
    return {
        "a_blocks": gaussian(arg_keys[0], (N_ROW, N_COL, BLOCK, CAPACITY * BLOCK), BLOCK ** -0.5, 0.75, ((0, 32), (1, 8))),
        "a_rows": set_ends(jax.random.randint(arg_keys[1], (N_ROW, N_COL, CAPACITY), 0, FINE_DEV), jax.random.fold_in(arg_keys[1], 1), 0, FINE_DEV - 1).astype(jnp.int32),
        "a_steps": set_ends(jax.random.randint(arg_keys[2], (N_ROW, N_COL, CAPACITY), 0, 3), jax.random.fold_in(arg_keys[2], 1), 0, 2).astype(jnp.int32),
        "a_cols": set_ends(jax.random.randint(arg_keys[3], (N_ROW, N_COL, CAPACITY), 0, SY + 2), jax.random.fold_in(arg_keys[3], 1), 0, (SY + 2) - 1).astype(jnp.int32),
        "a_live": draw_a_live(jax.random.fold_in(arg_keys[6], 71), 0),
        "p_blocks": gaussian(arg_keys[5], (NX, NY, BLOCK, SLOTS * BLOCK), 0.15, 0.8984375, ((0, 32), (1, 8))),
    }


def slot_targets(cell_x, cell_y, row_dev, span_x, span_y, aggr_count, row_count):
    owner_x = (cell_x + span_x) // span_x - 1
    owner_y = (cell_y + span_y) // span_y - 1
    local_u = cell_x - owner_x * span_x
    local_v = cell_y - owner_y * span_y
    band_id = local_v // (span_y // aggr_count)
    owner_row = row_dev + owner_x
    step_up = jnp.logical_and(local_u == span_x - 1, owner_row < row_count - 1).astype(jnp.int32)
    step_down = jnp.logical_and(local_u == 0, owner_row > 0).astype(jnp.int32)
    shift_x = step_up - step_down
    second_band = jnp.where(shift_x != 0, band_id, (band_id + 1) % aggr_count)
    offset_x = jnp.stack([owner_x, owner_x + shift_x], axis=-1)
    offset_y = jnp.stack([owner_y, owner_y], axis=-1)
    band_ids = jnp.stack([band_id, second_band], axis=-1)
    return offset_x, offset_y, band_ids


def block_layout(row_ids, step_ids, col_ids, row_dev, span_x, span_y, aggr_count, row_count):
    row_x = row_ids // span_y
    row_y = row_ids % span_y
    col_x = row_x + step_ids - 1
    outside = jnp.logical_or(col_x < 0, col_x >= span_x)
    col_y = jnp.where(outside, jnp.clip(col_ids - 1, 0, span_y - 1), col_ids - 1)
    ext_width = span_y + 2
    row_cell = (row_x + 1) * ext_width + row_y + 1
    col_cell = (col_x + 1) * ext_width + col_y + 1
    left_side = slot_targets(row_x, row_y, row_dev, span_x, span_y, aggr_count, row_count)
    right_side = slot_targets(col_x, col_y, row_dev, span_x, span_y, aggr_count, row_count)
    amount = row_ids.shape[0]
    group_ids = (right_side[0][:, None, :] - left_side[0][:, :, None] + 1) * 3 + right_side[1][:, None, :] + 1
    slot_part = jnp.broadcast_to(left_side[0][:, :, None] + 1, (amount, 2, 2))
    slot_row = jnp.broadcast_to(left_side[2][:, :, None], (amount, 2, 2))
    slot_col = group_ids * aggr_count + right_side[2][:, None, :]
    return row_cell, col_cell, slot_part, slot_row, slot_col


def reference(a_blocks, a_rows, a_steps, a_cols, a_live, p_blocks):
    padded = jnp.pad(p_blocks, ((1, 1), (1, 1), (0, 0), (0, 0)))
    out_rows = AGG_DEV * BLOCK
    out_cols = 9 * AGG_DEV * BLOCK
    cells = (SX + 2) * (SY + 2)

    def add_piece(summed, piece, row_at, col_at):
        start = (row_at, col_at, jnp.int32(0), jnp.int32(0))
        old = lax.dynamic_slice(summed, start, (1, 1, out_rows, out_cols))
        return lax.dynamic_update_slice(summed, old + piece[None, None], start)

    def device_term(summed, flat_index):
        row_dev = (flat_index // N_COL).astype(jnp.int32)
        col_dev = (flat_index % N_COL).astype(jnp.int32)
        window = lax.dynamic_slice(padded, (row_dev * SX, col_dev * SY, jnp.int32(0), jnp.int32(0)),
                                   (SX + 2, SY + 2, BLOCK, SLOTS * BLOCK))
        rows_table = window.reshape(cells, BLOCK, SLOTS * BLOCK).astype(jnp.float32)
        matrix = a_blocks[row_dev, col_dev].reshape(BLOCK, CAPACITY, BLOCK).astype(jnp.float32)
        row_cell, col_cell, slot_part, slot_row, slot_col = block_layout(
            a_rows[row_dev, col_dev], a_steps[row_dev, col_dev], a_cols[row_dev, col_dev],
            row_dev, SX, SY, AGG_DEV, N_ROW)
        left_rows = rows_table[row_cell]
        right_rows = rows_table[col_cell]
        product = jnp.einsum('xnb,nbk->nxk', matrix, right_rows)
        product = lax.optimization_barrier(product.astype(jnp.bfloat16)).astype(jnp.float32)
        contribs = jnp.einsum('nxsm,nxtk->nstmk',
                              left_rows.reshape(CAPACITY, BLOCK, SLOTS, BLOCK),
                              product.reshape(CAPACITY, BLOCK, SLOTS, BLOCK))
        keep_mask = (jnp.arange(CAPACITY, dtype=jnp.int32) < a_live[row_dev, col_dev]).astype(jnp.float32)
        contribs = contribs * keep_mask[:, None, None, None, None]
        partial_value = jnp.zeros((3, AGG_DEV, BLOCK, 9 * AGG_DEV, BLOCK), jnp.float32)
        partial_value = partial_value.at[slot_part.reshape(-1), slot_row.reshape(-1), :, slot_col.reshape(-1), :].add(
            contribs.reshape(-1, BLOCK, BLOCK))
        partial_value = partial_value.reshape(3, out_rows, out_cols)
        summed = add_piece(summed, partial_value[1], row_dev, col_dev)
        summed = add_piece(summed, partial_value[2], jnp.minimum(row_dev + 1, N_ROW - 1), col_dev)
        summed = add_piece(summed, partial_value[0], jnp.maximum(row_dev - 1, 0), col_dev)
        return summed, None

    start_sum = jnp.zeros((N_ROW, N_COL, out_rows, out_cols), jnp.float32)
    summed, _ = lax.scan(device_term, start_sum, jnp.arange(N_ROW * N_COL, dtype=jnp.int32))
    return summed.transpose(0, 2, 1, 3).reshape(N_ROW * out_rows, N_COL * out_cols)
```

```python
import functools

import jax
import jax.numpy as jnp
from jax import lax
from jax.experimental import pallas as pl
from jax.experimental.pallas import tpu as pltpu
from jax.sharding import PartitionSpec as P

B = 64
W2 = 128
SX, SY = 4, 64
FINE = SX * SY
HALF = SY // 2
TRASH_Z = 3 * FINE
N_WX = 128
N_W = N_WX + 32
TRASH_W = N_W
GROUP = 64
DEPTH = 4
FAR = 32
PT_STEPS = 1
UP_AT, DN_AT, SUMS = 3 * W2, 5 * W2, 7 * W2
SPARE_SUMS, SPARE_W = 144, 32
TAIL_VMEM = 24
MIB = 1024 * 1024
CHUNK = 128
f32, bf16 = jnp.float32, jnp.bfloat16


def swap_slots(x):
    return jnp.concatenate([x[..., B:], x[..., :B]], axis=-1)


def lanes_low(rows):
    return lax.broadcasted_iota(jnp.int32, (rows, W2), 1) < B


def roll(x):
    return pltpu.roll(x, B, 1)


def add_two(ref, i, j, x, y):
    old_i, old_j = ref[i], ref[j]
    new_i = old_i + x
    ref[i] = new_i
    ref[j] = jnp.where(i == j, new_i, old_j) + y


def main_kernel(scal, ci_ref, zi_ref, hp_ref, a_hbm, p_hbm,
                sums_hbm, wt_hbm,
                a_v, p_v, pt_v, z_v, w_v, stage, stage_y, sums, list_s, sem_a, sem_p, sem_w):
    capacity = hp_ref.shape[0]
    live = scal[0]
    first = scal[1]
    last = scal[2]

    p_copies = [pltpu.make_async_copy(p_hbm.at[pl.ds(u * SY, SY)], p_v.at[pl.ds(u * SY, SY)], sem_p.at[u])
                for u in range(SX)]
    for c in p_copies:
        c.start()

    def a_copy(k):
        at = pl.ds(pl.multiple_of(k * (CHUNK * B), CHUNK * B), CHUNK * B)
        return pltpu.make_async_copy(a_hbm.at[:, at], a_v.at[:, at], sem_a.at[k])

    used_chunks = (live + CHUNK - 1) // CHUNK

    @pl.loop(0, used_chunks)
    def _(k):
        a_copy(k).start()

    @functools.partial(lax.fori_loop, 0, 32, init_val=jnp.int32(0))
    def count(k, count):
        z_v[pl.ds(k * 24, 24)] = jnp.zeros((24, B, W2), f32)
        w_v[pl.ds(k * 5, 5)] = jnp.zeros((5, W2, W2), f32)
        for s in range(capacity // 32):
            h = hp_ref[k * (capacity // 32) + s]
            list_s[count] = h
            count = count + 1 + (h >> 31)
        return count

    for u in range(SX):
        p_copies[u].wait()
        for half in range(2):
            q = u * 2 + half
            flag = {0: first, SX - 1: last}.get(u)

            @pl.loop(0, PT_STEPS)
            def _(k):
                for s in range(16 // PT_STEPS):
                    t = k * (16 // PT_STEPS) + s
                    at = pl.ds(q * HALF + t * 2, 2)
                    pair = p_v[at]
                    if half == 1:
                        pair = swap_slots(pair) if flag is None else jnp.where(flag == 1, swap_slots(pair), pair)
                        p_v[at] = pair
                    pt_v[q * 16 + t] = pair.reshape(2 * B, W2).T

    for s in range(FAR):
        list_s[count + s] = jnp.int32(TRASH_W << 9)

    @pl.loop(0, used_chunks)
    def _(k):
        a_copy(k).wait()

    low = lanes_low(B)

    def far_dot(h):
        n = h >> 17
        par = (h >> 8) & 1
        r = h & 255
        a = a_v[:, pl.ds(pl.multiple_of((n >> 1) * W2, W2), W2)]
        a = jnp.where((n & 1) == par, a, swap_slots(a))
        a = jnp.where(low == (par == 0), a, jnp.zeros_like(a))
        even = (r & 1) == 0
        rhs = jnp.concatenate([jnp.where(even, a, jnp.zeros_like(a)),
                               jnp.where(even, jnp.zeros_like(a), a)], axis=0)
        return jnp.dot(pt_v[r >> 1], rhs, preferred_element_type=f32)

    @pl.loop(0, (count + FAR - 1) // FAR)
    def _(k):
        hs = [list_s[k * FAR + s] for s in range(FAR)]
        res = [far_dot(h) for h in hs]
        for s in range(0, FAR, 2):
            add_two(w_v, (hs[s] >> 9) & 255, (hs[s + 1] >> 9) & 255, res[s], res[s + 1])

    def w_copy(t):
        return pltpu.make_async_copy(
            stage.at[t], wt_hbm.at[t // 2, pl.ds((t % 2) * W2, W2)], sem_w.at[t])

    for t in range(4):
        @pl.loop(0, 32, unroll=8)
        def _(k):
            stage[t, :, pl.ds(pl.multiple_of(k * W2, W2), W2)] = w_v[t * 32 + k].astype(bf16)
        w_copy(t).start()

    @pl.loop(0, 32, unroll=8)
    def _(k):
        stage_y[:, pl.ds(pl.multiple_of(k * W2, W2), W2)] = w_v[N_WX + k].astype(bf16)

    y_copy = pltpu.make_async_copy(stage_y, wt_hbm.at[2, pl.ds(0, W2)], sem_w.at[4])
    y_copy.start()

    zero_p = jnp.zeros((B, W2), bf16)

    def near_dot(n):
        a = a_v[:, pl.ds(pl.multiple_of(n * B, W2), W2)]
        p0 = p_v[ci_ref[n]]
        p1 = p_v[ci_ref[n + 1]]
        w = jnp.concatenate([jnp.concatenate([p0, zero_p], axis=1),
                             jnp.concatenate([zero_p, p1], axis=1)], axis=0)
        return jnp.dot(a, w, preferred_element_type=f32)

    @pl.loop(0, (live + GROUP - 1) // GROUP)
    def _(g):
        n0 = g * GROUP
        res = {}
        for s in range(GROUP // 2 + DEPTH):
            if s < GROUP // 2:
                res[s] = near_dot(n0 + 2 * s)
            if s >= DEPTH:
                n, value = n0 + 2 * (s - DEPTH), res.pop(s - DEPTH)
                add_two(z_v, zi_ref[n], zi_ref[n + 1], value[:, :W2], value[:, W2:])

    low2 = lanes_low(W2)
    zb = jnp.zeros((B, W2), f32)
    for u in range(SX):
        mid = {0: first == 1, SX - 1: last == 1}.get(u)
        other = DN_AT if u == 0 else UP_AT
        for b in range(2):
            r0 = u * SY + b * HALF
            om = jnp.zeros((W2, W2), f32)
            oe = jnp.zeros((W2, 2 * W2), f32)
            for k in range(HALF // 4):
                r = r0 + 4 * k
                lhs = jnp.concatenate([pt_v[r // 2], pt_v[r // 2 + 1]], axis=1)
                zs = [z_v[pl.ds(g * FINE + r, 4)].reshape(4 * B, W2).astype(bf16) for g in range(3)]
                om += jnp.dot(lhs, zs[0], preferred_element_type=f32)
                oe += jnp.dot(lhs, jnp.concatenate(zs[1:], axis=1), preferred_element_type=f32)
            e0, e1 = oe[:, :W2], oe[:, W2:]
            same = om + jnp.where(low2, e0, roll(e1))
            adj = jnp.where(low2, roll(e0), e1)
            for g, c in ((1, same), (0 if u < 2 else 2, adj)):
                at = slice(g * W2, (g + 1) * W2)
                top, bot = c[:B], c[B:]
                if mid is not None:
                    slot = 0 if g == 1 else 1
                    sums[b * B:(b + 1) * B, other + slot * W2:other + (slot + 1) * W2] = jnp.where(mid, zb, bot)
                    bot = jnp.where(mid, bot, zb if b == 0 else top)
                    top = top if b == 0 else jnp.where(mid, top, zb)
                if b == 0 and (u == 0 or (u == 2 and g == 2)):
                    sums[:B, at] = top
                    sums[B:, at] = bot
                else:
                    sums[:B, at] += top
                    sums[B:, at] += bot

    out_copy = pltpu.make_async_copy(sums, sums_hbm.at[0], sem_w.at[5])
    out_copy.start()
    for t in range(4):
        w_copy(t).wait()
    y_copy.wait()
    out_copy.wait()


def tail_kernel(scal, sums_hbm, wt_hbm, yl_ref, yr_ref, hu_ref, hd_ref,
                own_ref, up_ref, dn_ref, sums, wy_ref, wt_ref, sem, sem_w):
    first, last, has_l, has_r = scal[1], scal[2], scal[3], scal[4]
    copies = [pltpu.make_async_copy(src, dst, sem.at[k]) for k, (src, dst) in enumerate(
        ((wt_hbm.at[2, pl.ds(0, W2)], wy_ref), (sums_hbm.at[0], sums)))]
    for c in copies:
        c.start()
    w_copies = [pltpu.make_async_copy(wt_hbm.at[t // 2, pl.ds((t % 2) * W2, W2)],
                                      wt_ref.at[t // 2, pl.ds((t % 2) * W2, W2)], sem_w.at[t]) for t in range(4)]
    for c in w_copies:
        c.start()

    low = lanes_low(W2)
    zl = jnp.zeros((B, W2), bf16)
    zt = jnp.zeros((W2, W2), f32)
    zb = jnp.zeros((B, W2), f32)
    rhs_y, is_mid = [], []
    for u in range(SX):
        mid = {0: first == 1, SX - 1: last == 1}.get(u)
        left = jnp.where(has_l == 1, yl_ref[u, 0], zl)
        right = jnp.where(has_r == 1, yr_ref[u, 0], zl)
        swapped = swap_slots(left)
        left = swapped if mid is None else jnp.where(mid, swapped, left)
        rhs_y.append(jnp.concatenate([jnp.concatenate([left, zl], axis=1),
                                      jnp.concatenate([zl, right], axis=1)], axis=0))
        is_mid.append(mid)
    for g in range(3):
        for k in (3 * g, 3 * g + 2):
            own_ref[:, k * W2:(k + 1) * W2] = zt

    copies[0].wait()
    for u in range(SX):
        mid = is_mid[u]
        other = dn_ref if u == 0 else up_ref
        for b in range(2):
            same = {-1: zt, 1: zt}
            adj = {-1: zt, 1: zt}
            for uc in range(max(0, u - 1), min(SX, u + 2)):
                k = uc * 8 + u * 2 + b
                ty = jnp.dot(wy_ref[:, k * W2:(k + 1) * W2], rhs_y[uc], preferred_element_type=f32)
                tl, tr = ty[:, :W2], ty[:, W2:]
                stays = is_mid[uc]
                if stays is None:
                    same[-1] += tl
                    same[1] += tr
                else:
                    same[-1] += jnp.where(stays, tl, jnp.where(low, zt, roll(tl)))
                    same[1] += jnp.where(stays, tr, jnp.where(low, tr, zt))
                    adj[-1] += jnp.where(stays, zt, jnp.where(low, zt, tl))
                    adj[1] += jnp.where(stays, zt, jnp.where(low, roll(tr), zt))
            adj_dx = 0 if u < 2 else 2
            for dy in (-1, 1):
                for dx, c in ((1, same[dy]), (adj_dx, adj[dy])):
                    at = slice((dx * 3 + dy + 1) * W2, (dx * 3 + dy + 2) * W2)
                    top, bot = c[:B], c[B:]
                    if mid is not None:
                        bot = jnp.where(mid, bot, zb if b == 0 else top)
                        top = top if b == 0 else jnp.where(mid, top, zb)
                    own_ref[:B, at] += top
                    own_ref[B:, at] += bot
            if mid is not None:
                q = slice(b * B, (b + 1) * B)
                for slot, c in ((2, same[-1]), (3, same[1]), (4, adj[-1] + adj[1])):
                    other[q, slot * W2:(slot + 1) * W2] = jnp.where(mid, zb, c[B:]).astype(bf16)

    for c in copies[1:]:
        c.wait()
    low2 = lanes_low(2 * W2)
    middle = [sums[:, dx * W2:(dx + 1) * W2] for dx in range(3)]
    for side, halo, valid, src, dst in ((0, hd_ref, first == 0, DN_AT, dn_ref), (1, hu_ref, last == 0, UP_AT, up_ref)):
        w_copies[2 * side].wait()
        w_copies[2 * side + 1].wait()
        t = []
        for b in range(2):
            rhs = halo[b * HALF:(b + 1) * HALF].reshape(HALF * B, W2)
            lhs = wt_ref[side, :, b * HALF * B:(b + 1) * HALF * B]
            out = jnp.dot(lhs, rhs, preferred_element_type=f32)
            t.append(jnp.where(valid, out, jnp.zeros_like(out)))
        same = jnp.where(low2, roll(t[0]), t[1])
        adj = jnp.where(low2, t[0], roll(t[1]))
        dx = 0 if side == 0 else 2
        middle[1] = middle[1] + jnp.concatenate([same[:B], same[W2:W2 + B]], axis=0)
        middle[dx] = middle[dx] + jnp.concatenate([adj[:B], adj[W2:W2 + B]], axis=0)
        away = [jnp.concatenate([x[B:W2], x[W2 + B:]], axis=0) for x in (same, adj)]
        for k in range(2):
            dst[:, k * W2:(k + 1) * W2] = (sums[:, src + k * W2:src + (k + 1) * W2] + away[k]).astype(bf16)
    for dx in range(3):
        own_ref[:, (3 * dx + 1) * W2:(3 * dx + 2) * W2] = middle[dx]


def edges_kernel(p_hbm, up_ref, dn_ref, yr_ref, yl_ref, sem):
    copies = [pltpu.make_async_copy(src, dst, sem.at[k]) for k, (src, dst) in enumerate((
        (p_hbm.at[SX - 1], up_ref), (p_hbm.at[0], dn_ref),
        (p_hbm.at[:, pl.ds(SY - 1, 1)], yr_ref), (p_hbm.at[:, pl.ds(0, 1)], yl_ref)))]
    for c in copies:
        c.start()
    for c in copies:
        c.wait()


def final_kernel(scal, own_ref, below_ref, above_ref, out_ref):
    low = lanes_low(W2)
    zero = jnp.zeros((W2, W2), f32)
    has_below = scal[1] == 0
    has_above = scal[2] == 0

    def piece(ref, k, valid):
        return jnp.where(valid, ref[:, k * W2:(k + 1) * W2].astype(f32), zero)

    lo = [piece(below_ref, k, has_below) for k in range(5)]
    hi = [piece(above_ref, k, has_above) for k in range(5)]
    sides = lo[4] + hi[4]
    extra = {
        0: lo[2], 1: lo[0], 2: lo[3],
        3: jnp.where(low, zero, sides), 4: lo[1] + hi[1], 5: jnp.where(low, sides, zero),
        6: hi[2], 7: hi[0], 8: hi[3],
    }
    for k, value in extra.items():
        out_ref[:, k * W2:(k + 1) * W2] = own_ref[:, k * W2:(k + 1) * W2] + value


def layout(rows, steps, cols, live, first, last):
    n = jnp.arange(rows.shape[0], dtype=jnp.int32)
    ur, br = rows // SY, (rows % SY) // HALF
    cx = ur + steps - 1
    outside = jnp.logical_or(cx < 0, cx >= SX)
    cy = jnp.where(outside, jnp.clip(cols - 1, 0, SY - 1), cols - 1)
    beside = jnp.logical_and(jnp.logical_not(outside), jnp.logical_or(cy < 0, cy >= SY))
    here = n < live
    far = jnp.logical_or(outside, beside)
    near = jnp.logical_and(here, jnp.logical_not(far))
    edge = jnp.logical_or(jnp.logical_and(cx == 0, first == 0), jnp.logical_and(cx == SX - 1, last == 0))
    kind = jnp.where(edge, 1 + cy // HALF, 0)
    ci = jnp.where(near, cx * SY + cy, 0)
    zi = jnp.where(near, kind * FINE + rows, TRASH_Z)
    side = (cx >= SX).astype(jnp.int32)
    y_side = (cy >= SY).astype(jnp.int32)
    wi = jnp.where(outside, (side * 2 + br) * HALF + cy // 2, N_WX + cx * 8 + ur * 2 + br)
    par = jnp.where(outside, cy % 2, y_side)
    hp = jnp.where(jnp.logical_and(here, far), (n << 17) | (wi << 9) | (par << 8) | rows, -1)
    return ci, zi, hp


def on_device(a_blocks, a_rows, a_steps, a_cols, a_live, p_blocks):
    capacity = a_rows.shape[2]
    n_row, n_col = lax.axis_size("row"), lax.axis_size("col")
    i, j = lax.axis_index("row"), lax.axis_index("col")

    def ring(x, axis, step):
        n = lax.axis_size(axis)
        return lax.ppermute(x, axis, [(k, (k + step) % n) for k in range(n)])

    smem = pl.BlockSpec(memory_space=pltpu.SMEM)
    vmem = pl.BlockSpec(memory_space=pltpu.VMEM)
    hbm = pl.BlockSpec(memory_space=pl.ANY)
    row = jax.ShapeDtypeStruct((SY, B, W2), bf16)
    column = jax.ShapeDtypeStruct((SX, 1, B, W2), bf16)
    p_last, p_first, p_right, p_left = pl.pallas_call(
        edges_kernel,
        in_specs=[hbm],
        out_specs=[vmem] * 4,
        out_shape=[row, row, column, column],
        scratch_shapes=[pltpu.SemaphoreType.DMA((4,))],
        compiler_params=pltpu.CompilerParams(vmem_limit_bytes=60 * MIB),
        name="edges",
    )(p_blocks)
    halo_dn = ring(p_last, "row", 1)
    halo_up = ring(p_first, "row", -1)
    y_left = ring(p_right, "col", 1)
    y_right = ring(p_left, "col", -1)

    live = a_live.reshape(())
    first = (i == 0).astype(jnp.int32)
    last = (i == n_row - 1).astype(jnp.int32)
    scal = jnp.stack([live, first, last, (j > 0).astype(jnp.int32), (j < n_col - 1).astype(jnp.int32)])
    ci, zi, hp = layout(a_rows.reshape(-1), a_steps.reshape(-1), a_cols.reshape(-1), live, first, last)

    sums, wt = pl.pallas_call(
        main_kernel,
        in_specs=[smem, smem, smem, smem, hbm, hbm],
        out_specs=[hbm, hbm],
        out_shape=[
            jax.ShapeDtypeStruct((SPARE_SUMS, W2, SUMS), f32),
            jax.ShapeDtypeStruct((SPARE_W, 2 * W2, SY * B), bf16),
        ],
        scratch_shapes=[
            pltpu.VMEM((B, capacity * B), bf16),
            pltpu.VMEM((FINE, B, W2), bf16),
            pltpu.VMEM((FINE // 2, W2, W2), bf16),
            pltpu.VMEM((TRASH_Z + 1, B, W2), f32),
            pltpu.VMEM((N_W + 1, W2, W2), f32),
            pltpu.VMEM((4, W2, SY * B), bf16),
            pltpu.VMEM((W2, 32 * W2), bf16),
            pltpu.VMEM((W2, SUMS), f32),
            pltpu.SMEM((capacity + FAR,), jnp.int32),
            pltpu.SemaphoreType.DMA((capacity // CHUNK,)),
            pltpu.SemaphoreType.DMA((SX,)),
            pltpu.SemaphoreType.DMA((6,)),
        ],
        compiler_params=pltpu.CompilerParams(vmem_limit_bytes=60 * MIB),
        cost_estimate=pl.CostEstimate(flops=4_000_000_000, bytes_accessed=20_000_000, transcendentals=0),
        name="galerkin_main",
    )(scal, ci, zi, hp, a_blocks.reshape(B, capacity * B), p_blocks.reshape(FINE, B, W2))

    own, up, dn = pl.pallas_call(
        tail_kernel,
        in_specs=[smem] + [hbm] * 2 + [vmem] * 4,
        out_specs=[vmem] * 3,
        out_shape=[
            jax.ShapeDtypeStruct((W2, 9 * W2), f32),
            jax.ShapeDtypeStruct((W2, 5 * W2), bf16),
            jax.ShapeDtypeStruct((W2, 5 * W2), bf16),
        ],
        scratch_shapes=[
            pltpu.VMEM((W2, SUMS), f32),
            pltpu.VMEM((W2, 32 * W2), bf16),
            pltpu.VMEM((2, 2 * W2, SY * B), bf16),
            pltpu.SemaphoreType.DMA((4,)),
            pltpu.SemaphoreType.DMA((4,)),
        ],
        compiler_params=pltpu.CompilerParams(vmem_limit_bytes=TAIL_VMEM * MIB),
        cost_estimate=pl.CostEstimate(flops=800_000_000, bytes_accessed=8_000_000, transcendentals=0),
        name="galerkin_halo",
    )(scal, sums, wt, y_left, y_right, halo_up, halo_dn)

    from_below = ring(up, "row", 1)
    from_above = ring(dn, "row", -1)

    return pl.pallas_call(
        final_kernel,
        in_specs=[smem] + [vmem] * 3,
        out_specs=vmem,
        out_shape=jax.ShapeDtypeStruct((W2, 9 * W2), f32),
        compiler_params=pltpu.CompilerParams(vmem_limit_bytes=8 * MIB),
        name="galerkin_sum",
    )(scal, own, from_below, from_above)


def solution(mesh):
    return jax.shard_map(
        on_device,
        mesh=mesh,
        in_specs=(
            P("row", "col", None, None),
            P("row", "col", None),
            P("row", "col", None),
            P("row", "col", None),
            P("row", "col"),
            P("row", "col", None, None),
        ),
        out_specs=P("row", "col"),
        check_vma=False,
    )
```

```python
import functools

import jax
import jax.numpy as jnp
from jax import lax
from jax.experimental import pallas as pl
from jax.experimental.pallas import tpu as pltpu
from jax.sharding import PartitionSpec as P

B = 64
W2 = 128
SX, SY = 4, 64
FINE = SX * SY
HALF = SY // 2
TRASH_Z = 3 * FINE
N_WX = 128
N_W = N_WX + 32
TRASH_W = N_W
GROUP = 64
DEPTH = 4
FAR = 32
PT_STEPS = 1
UP_AT, DN_AT, SUMS = 3 * W2, 5 * W2, 7 * W2
SPARE_SUMS, SPARE_W = 144, 32
TAIL_VMEM = 24
MIB = 1024 * 1024
CHUNK = 128
f32, bf16 = jnp.float32, jnp.bfloat16


def swap_slots(x):
    return jnp.concatenate([x[..., B:], x[..., :B]], axis=-1)


def lanes_low(rows):
    return lax.broadcasted_iota(jnp.int32, (rows, W2), 1) < B


def place(axis):
    i = lax.axis_index(axis)
    return i == 0, i == lax.axis_size(axis) - 1, i % 2 == 0


def roll(x):
    return pltpu.roll(x, B, 1)


def add_two(ref, i, j, x, y):
    old_i, old_j = ref[i], ref[j]
    new_i = old_i + x
    ref[i] = new_i
    ref[j] = jnp.where(i == j, new_i, old_j) + y


def main_kernel(live_ref, ci_ref, zi_ref, hp_ref, a_hbm, p_hbm,
                sums_hbm, wt_hbm,
                a_v, p_v, pt_v, z_v, w_v, stage, stage_y, sums, list_s, sem_a, sem_p, sem_w):
    capacity = hp_ref.shape[0]
    live = live_ref[0, 0]
    first, last, _ = place("row")

    p_copies = [pltpu.make_async_copy(p_hbm.at[pl.ds(u * SY, SY)], p_v.at[pl.ds(u * SY, SY)], sem_p.at[u])
                for u in range(SX)]
    for c in p_copies:
        c.start()

    def a_copy(k):
        at = pl.ds(pl.multiple_of(k * (CHUNK * B), CHUNK * B), CHUNK * B)
        return pltpu.make_async_copy(a_hbm.at[:, at], a_v.at[:, at], sem_a.at[k])

    used_chunks = (live + CHUNK - 1) // CHUNK

    @pl.loop(0, used_chunks)
    def _(k):
        a_copy(k).start()

    @functools.partial(lax.fori_loop, 0, 32, init_val=jnp.int32(0))
    def count(k, count):
        z_v[pl.ds(k * 24, 24)] = jnp.zeros((24, B, W2), f32)
        w_v[pl.ds(k * 5, 5)] = jnp.zeros((5, W2, W2), f32)
        for s in range(capacity // 32):
            h = hp_ref[k * (capacity // 32) + s]
            list_s[count] = h
            count = count + 1 + (h >> 31)
        return count

    for u in range(SX):
        p_copies[u].wait()
        for half in range(2):
            q = u * 2 + half
            flag = {0: first, SX - 1: last}.get(u)

            @pl.loop(0, PT_STEPS)
            def _(k):
                for s in range(16 // PT_STEPS):
                    t = k * (16 // PT_STEPS) + s
                    at = pl.ds(q * HALF + t * 2, 2)
                    pair = p_v[at]
                    if half == 1:
                        pair = swap_slots(pair) if flag is None else jnp.where(flag, swap_slots(pair), pair)
                        p_v[at] = pair
                    pt_v[q * 16 + t] = pair.reshape(2 * B, W2).T

    for s in range(FAR):
        list_s[count + s] = jnp.int32(TRASH_W << 9)

    @pl.loop(0, used_chunks)
    def _(k):
        a_copy(k).wait()

    low = lanes_low(B)

    def far_dot(h):
        n = h >> 17
        par = (h >> 8) & 1
        r = h & 255
        a = a_v[:, pl.ds(pl.multiple_of((n >> 1) * W2, W2), W2)]
        a = jnp.where((n & 1) == par, a, swap_slots(a))
        a = jnp.where(low == (par == 0), a, jnp.zeros_like(a))
        even = (r & 1) == 0
        rhs = jnp.concatenate([jnp.where(even, a, jnp.zeros_like(a)),
                               jnp.where(even, jnp.zeros_like(a), a)], axis=0)
        return jnp.dot(pt_v[r >> 1], rhs, preferred_element_type=f32)

    @pl.loop(0, (count + FAR - 1) // FAR)
    def _(k):
        hs = [list_s[k * FAR + s] for s in range(FAR)]
        res = [far_dot(h) for h in hs]
        for s in range(0, FAR, 2):
            add_two(w_v, (hs[s] >> 9) & 255, (hs[s + 1] >> 9) & 255, res[s], res[s + 1])

    def w_copy(t):
        return pltpu.make_async_copy(
            stage.at[t], wt_hbm.at[t // 2, pl.ds((t % 2) * W2, W2)], sem_w.at[t])

    for t in range(4):
        @pl.loop(0, 32, unroll=8)
        def _(k):
            stage[t, :, pl.ds(pl.multiple_of(k * W2, W2), W2)] = w_v[t * 32 + k].astype(bf16)
        w_copy(t).start()

    @pl.loop(0, 32, unroll=8)
    def _(k):
        stage_y[:, pl.ds(pl.multiple_of(k * W2, W2), W2)] = w_v[N_WX + k].astype(bf16)

    y_copy = pltpu.make_async_copy(stage_y, wt_hbm.at[2, pl.ds(0, W2)], sem_w.at[4])
    y_copy.start()

    zero_p = jnp.zeros((B, W2), bf16)

    def near_dot(n):
        a = a_v[:, pl.ds(pl.multiple_of(n * B, W2), W2)]
        p0 = p_v[ci_ref[n]]
        p1 = p_v[ci_ref[n + 1]]
        w = jnp.concatenate([jnp.concatenate([p0, zero_p], axis=1),
                             jnp.concatenate([zero_p, p1], axis=1)], axis=0)
        return jnp.dot(a, w, preferred_element_type=f32)

    @pl.loop(0, (live + GROUP - 1) // GROUP)
    def _(g):
        n0 = g * GROUP
        res = {}
        for s in range(GROUP // 2 + DEPTH):
            if s < GROUP // 2:
                res[s] = near_dot(n0 + 2 * s)
            if s >= DEPTH:
                n, value = n0 + 2 * (s - DEPTH), res.pop(s - DEPTH)
                add_two(z_v, zi_ref[n], zi_ref[n + 1], value[:, :W2], value[:, W2:])

    low2 = lanes_low(W2)
    zb = jnp.zeros((B, W2), f32)
    for u in range(SX):
        mid = {0: first, SX - 1: last}.get(u)
        other = DN_AT if u == 0 else UP_AT
        for b in range(2):
            r0 = u * SY + b * HALF
            om = jnp.zeros((W2, W2), f32)
            oe = jnp.zeros((W2, 2 * W2), f32)
            for k in range(HALF // 4):
                r = r0 + 4 * k
                lhs = jnp.concatenate([pt_v[r // 2], pt_v[r // 2 + 1]], axis=1)
                zs = [z_v[pl.ds(g * FINE + r, 4)].reshape(4 * B, W2).astype(bf16) for g in range(3)]
                om += jnp.dot(lhs, zs[0], preferred_element_type=f32)
                oe += jnp.dot(lhs, jnp.concatenate(zs[1:], axis=1), preferred_element_type=f32)
            e0, e1 = oe[:, :W2], oe[:, W2:]
            same = om + jnp.where(low2, e0, roll(e1))
            adj = jnp.where(low2, roll(e0), e1)
            for g, c in ((1, same), (0 if u < 2 else 2, adj)):
                at = slice(g * W2, (g + 1) * W2)
                top, bot = c[:B], c[B:]
                if mid is not None:
                    slot = 0 if g == 1 else 1
                    sums[b * B:(b + 1) * B, other + slot * W2:other + (slot + 1) * W2] = jnp.where(mid, zb, bot)
                    bot = jnp.where(mid, bot, zb if b == 0 else top)
                    top = top if b == 0 else jnp.where(mid, top, zb)
                if b == 0 and (u == 0 or (u == 2 and g == 2)):
                    sums[:B, at] = top
                    sums[B:, at] = bot
                else:
                    sums[:B, at] += top
                    sums[B:, at] += bot

    out_copy = pltpu.make_async_copy(sums, sums_hbm.at[0], sem_w.at[5])
    out_copy.start()
    for t in range(4):
        w_copy(t).wait()
    y_copy.wait()
    out_copy.wait()


def beside_kernel(sums_hbm, wt_hbm, yl_ref, yr_ref,
                  own_ref, up_ref, dn_ref, wt_ref, sums, wy_ref, sem, sem_w):
    first, last, _ = place("row")
    no_l, no_r, _ = place("col")
    copies = [pltpu.make_async_copy(src, dst, sem.at[k]) for k, (src, dst) in enumerate(
        ((wt_hbm.at[2, pl.ds(0, W2)], wy_ref), (sums_hbm.at[0], sums)))]
    for c in copies:
        c.start()
    w_copies = [pltpu.make_async_copy(wt_hbm.at[t // 2, pl.ds((t % 2) * W2, W2)],
                                      wt_ref.at[t // 2, pl.ds((t % 2) * W2, W2)], sem_w.at[t]) for t in range(4)]
    for c in w_copies:
        c.start()

    low = lanes_low(W2)
    zl = jnp.zeros((B, W2), bf16)
    zt = jnp.zeros((W2, W2), f32)
    zb = jnp.zeros((B, W2), f32)
    rhs_y, is_mid = [], []
    for u in range(SX):
        mid = {0: first, SX - 1: last}.get(u)
        left = jnp.where(no_l, zl, yl_ref[u, 0])
        right = jnp.where(no_r, zl, yr_ref[u, 0])
        swapped = swap_slots(left)
        left = swapped if mid is None else jnp.where(mid, swapped, left)
        rhs_y.append(jnp.concatenate([jnp.concatenate([left, zl], axis=1),
                                      jnp.concatenate([zl, right], axis=1)], axis=0))
        is_mid.append(mid)
    for g in range(3):
        for k in (3 * g, 3 * g + 2):
            own_ref[:, k * W2:(k + 1) * W2] = zt

    copies[0].wait()
    for u in range(SX):
        mid = is_mid[u]
        other = dn_ref if u == 0 else up_ref
        for b in range(2):
            same = {-1: zt, 1: zt}
            adj = {-1: zt, 1: zt}
            for uc in range(max(0, u - 1), min(SX, u + 2)):
                k = uc * 8 + u * 2 + b
                ty = jnp.dot(wy_ref[:, k * W2:(k + 1) * W2], rhs_y[uc], preferred_element_type=f32)
                tl, tr = ty[:, :W2], ty[:, W2:]
                stays = is_mid[uc]
                if stays is None:
                    same[-1] += tl
                    same[1] += tr
                else:
                    same[-1] += jnp.where(stays, tl, jnp.where(low, zt, roll(tl)))
                    same[1] += jnp.where(stays, tr, jnp.where(low, tr, zt))
                    adj[-1] += jnp.where(stays, zt, jnp.where(low, zt, tl))
                    adj[1] += jnp.where(stays, zt, jnp.where(low, roll(tr), zt))
            adj_dx = 0 if u < 2 else 2
            for dy in (-1, 1):
                for dx, c in ((1, same[dy]), (adj_dx, adj[dy])):
                    at = slice((dx * 3 + dy + 1) * W2, (dx * 3 + dy + 2) * W2)
                    top, bot = c[:B], c[B:]
                    if mid is not None:
                        bot = jnp.where(mid, bot, zb if b == 0 else top)
                        top = top if b == 0 else jnp.where(mid, top, zb)
                    own_ref[:B, at] += top
                    own_ref[B:, at] += bot
            if mid is not None:
                q = slice(b * B, (b + 1) * B)
                for slot, c in ((2, same[-1]), (3, same[1]), (4, adj[-1] + adj[1])):
                    other[q, slot * W2:(slot + 1) * W2] = jnp.where(mid, zb, c[B:])

    copies[1].wait()
    for dx in range(3):
        own_ref[:, (3 * dx + 1) * W2:(3 * dx + 2) * W2] = sums[:, dx * W2:(dx + 1) * W2]
    up_ref[:, :2 * W2] = sums[:, UP_AT:DN_AT]
    dn_ref[:, :2 * W2] = sums[:, DN_AT:]
    for c in w_copies:
        c.wait()


def tail_kernel(own_in, up_in, dn_in, wt_ref, ha_ref, hb_ref, own_ref, oa_ref, ob_ref):
    first, last, even = place("row")
    low = lanes_low(2 * W2)
    middle = [own_in[:, (3 * dx + 1) * W2:(3 * dx + 2) * W2] for dx in range(3)]
    away = []
    for side, valid, src in ((0, jnp.logical_not(first), dn_in), (1, jnp.logical_not(last), up_in)):
        t = []
        for b in range(2):
            near = slice(b * HALF, (b + 1) * HALF)
            one, two = (ha_ref, hb_ref) if side == 1 else (hb_ref, ha_ref)
            rhs = jnp.where(even, one[near], two[near]).reshape(HALF * B, W2)
            lhs = wt_ref[side, :, b * HALF * B:(b + 1) * HALF * B]
            out = jnp.dot(lhs, rhs, preferred_element_type=f32)
            t.append(jnp.where(valid, out, jnp.zeros_like(out)))
        same = jnp.where(low, roll(t[0]), t[1])
        adj = jnp.where(low, t[0], roll(t[1]))
        dx = 0 if side == 0 else 2
        middle[1] = middle[1] + jnp.concatenate([same[:B], same[W2:W2 + B]], axis=0)
        middle[dx] = middle[dx] + jnp.concatenate([adj[:B], adj[W2:W2 + B]], axis=0)
        parts = [src[:, k * W2:(k + 1) * W2] for k in range(5)]
        for k, x in enumerate((same, adj)):
            parts[k] = parts[k] + jnp.concatenate([x[B:W2], x[W2 + B:]], axis=0)
        away.append(parts)
    for k in range(5):
        at = slice(k * W2, (k + 1) * W2)
        oa_ref[:, at] = jnp.where(even, away[1][k], away[0][k]).astype(bf16)
        ob_ref[:, at] = jnp.where(even, away[0][k], away[1][k]).astype(bf16)
    for dx in range(3):
        own_ref[:, (3 * dx + 1) * W2:(3 * dx + 2) * W2] = middle[dx]
        for dy in (0, 2):
            at = slice((3 * dx + dy) * W2, (3 * dx + dy + 1) * W2)
            own_ref[:, at] = own_in[:, at]


def edges_kernel(p_hbm, xa_ref, xb_ref, yr_ref, yl_ref, sem):
    _, _, even = place("row")
    to_a = jnp.where(even, SX - 1, 0)
    copies = [pltpu.make_async_copy(src, dst, sem.at[k]) for k, (src, dst) in enumerate((
        (p_hbm.at[to_a], xa_ref), (p_hbm.at[SX - 1 - to_a], xb_ref),
        (p_hbm.at[:, pl.ds(SY - 1, 1)], yr_ref), (p_hbm.at[:, pl.ds(0, 1)], yl_ref)))]
    for c in copies:
        c.start()
    for c in copies:
        c.wait()


def final_kernel(own_ref, ra_ref, rb_ref, out_ref):
    first, last, even = place("row")
    low = lanes_low(W2)
    zero = jnp.zeros((W2, W2), f32)
    a = [ra_ref[:, k * W2:(k + 1) * W2].astype(f32) for k in range(5)]
    b = [rb_ref[:, k * W2:(k + 1) * W2].astype(f32) for k in range(5)]
    lo = [jnp.where(first, zero, jnp.where(even, y, x)) for x, y in zip(a, b)]
    hi = [jnp.where(last, zero, jnp.where(even, x, y)) for x, y in zip(a, b)]
    sides = lo[4] + hi[4]
    extra = {
        0: lo[2], 1: lo[0], 2: lo[3],
        3: jnp.where(low, zero, sides), 4: lo[1] + hi[1], 5: jnp.where(low, sides, zero),
        6: hi[2], 7: hi[0], 8: hi[3],
    }
    for k, value in extra.items():
        out_ref[:, k * W2:(k + 1) * W2] = own_ref[:, k * W2:(k + 1) * W2] + value


def layout(rows, steps, cols, live, first, last):
    n = jnp.arange(rows.shape[0], dtype=jnp.int32)
    ur, br = rows // SY, (rows % SY) // HALF
    cx = ur + steps - 1
    outside = jnp.logical_or(cx < 0, cx >= SX)
    cy = jnp.where(outside, jnp.clip(cols - 1, 0, SY - 1), cols - 1)
    beside = jnp.logical_and(jnp.logical_not(outside), jnp.logical_or(cy < 0, cy >= SY))
    here = n < live
    far = jnp.logical_or(outside, beside)
    near = jnp.logical_and(here, jnp.logical_not(far))
    edge = jnp.logical_or(jnp.logical_and(cx == 0, first == 0), jnp.logical_and(cx == SX - 1, last == 0))
    kind = jnp.where(edge, 1 + cy // HALF, 0)
    ci = jnp.where(near, cx * SY + cy, 0)
    zi = jnp.where(near, kind * FINE + rows, TRASH_Z)
    side = (cx >= SX).astype(jnp.int32)
    y_side = (cy >= SY).astype(jnp.int32)
    wi = jnp.where(outside, (side * 2 + br) * HALF + cy // 2, N_WX + cx * 8 + ur * 2 + br)
    par = jnp.where(outside, cy % 2, y_side)
    hp = jnp.where(jnp.logical_and(here, far), (n << 17) | (wi << 9) | (par << 8) | rows, -1)
    return ci, zi, hp


def on_device(a_blocks, a_rows, a_steps, a_cols, a_live, p_blocks):
    capacity = a_rows.shape[2]
    n_row = lax.axis_size("row")
    i = lax.axis_index("row")

    def ring(x, axis, step):
        n = lax.axis_size(axis)
        return lax.ppermute(x, axis, [(k, (k + step) % n) for k in range(n)])

    pairs_a = [(k, min(k ^ 1, n_row - 1)) for k in range(n_row)]
    pairs_b = [(k, min(max(((k + 1) ^ 1) - 1, 0), n_row - 1)) for k in range(n_row)]

    smem = pl.BlockSpec(memory_space=pltpu.SMEM)
    vmem = pl.BlockSpec(memory_space=pltpu.VMEM)
    hbm = pl.BlockSpec(memory_space=pl.ANY)
    row = jax.ShapeDtypeStruct((SY, B, W2), bf16)
    column = jax.ShapeDtypeStruct((SX, 1, B, W2), bf16)
    x_a, x_b, p_right, p_left = pl.pallas_call(
        edges_kernel,
        in_specs=[hbm],
        out_specs=[hbm] * 4,
        out_shape=[row, row, column, column],
        scratch_shapes=[pltpu.SemaphoreType.DMA((4,))],
        compiler_params=pltpu.CompilerParams(vmem_limit_bytes=52 * MIB),
        name="edges",
    )(p_blocks)
    halo_a = lax.ppermute(x_a, "row", pairs_a)
    halo_b = lax.ppermute(x_b, "row", pairs_b)
    y_left = ring(p_right, "col", 1)
    y_right = ring(p_left, "col", -1)

    live = a_live.reshape(())
    first = (i == 0).astype(jnp.int32)
    last = (i == n_row - 1).astype(jnp.int32)
    ci, zi, hp = layout(a_rows.reshape(-1), a_steps.reshape(-1), a_cols.reshape(-1), live, first, last)

    sums, wt = pl.pallas_call(
        main_kernel,
        in_specs=[smem, smem, smem, smem, hbm, hbm],
        out_specs=[hbm, hbm],
        out_shape=[
            jax.ShapeDtypeStruct((SPARE_SUMS, W2, SUMS), f32),
            jax.ShapeDtypeStruct((SPARE_W, 2 * W2, SY * B), bf16),
        ],
        scratch_shapes=[
            pltpu.VMEM((B, capacity * B), bf16),
            pltpu.VMEM((FINE, B, W2), bf16),
            pltpu.VMEM((FINE // 2, W2, W2), bf16),
            pltpu.VMEM((TRASH_Z + 1, B, W2), f32),
            pltpu.VMEM((N_W + 1, W2, W2), f32),
            pltpu.VMEM((4, W2, SY * B), bf16),
            pltpu.VMEM((W2, 32 * W2), bf16),
            pltpu.VMEM((W2, SUMS), f32),
            pltpu.SMEM((capacity + FAR,), jnp.int32),
            pltpu.SemaphoreType.DMA((capacity // CHUNK,)),
            pltpu.SemaphoreType.DMA((SX,)),
            pltpu.SemaphoreType.DMA((6,)),
        ],
        compiler_params=pltpu.CompilerParams(vmem_limit_bytes=60 * MIB),
        cost_estimate=pl.CostEstimate(flops=4_000_000_000, bytes_accessed=20_000_000, transcendentals=0),
        name="galerkin_main",
    )(a_live, ci, zi, hp, a_blocks.reshape(B, capacity * B), p_blocks.reshape(FINE, B, W2))

    own_shape = jax.ShapeDtypeStruct((W2, 9 * W2), f32)
    own, up, dn, wt = pl.pallas_call(
        beside_kernel,
        in_specs=[hbm] * 2 + [vmem] * 2,
        out_specs=[vmem] * 4,
        out_shape=[
            own_shape,
            jax.ShapeDtypeStruct((W2, 5 * W2), f32),
            jax.ShapeDtypeStruct((W2, 5 * W2), f32),
            jax.ShapeDtypeStruct((2, 2 * W2, SY * B), bf16),
        ],
        scratch_shapes=[
            pltpu.VMEM((W2, SUMS), f32),
            pltpu.VMEM((W2, 32 * W2), bf16),
            pltpu.SemaphoreType.DMA((2,)),
            pltpu.SemaphoreType.DMA((4,)),
        ],
        compiler_params=pltpu.CompilerParams(vmem_limit_bytes=TAIL_VMEM * MIB),
        cost_estimate=pl.CostEstimate(flops=200_000_000, bytes_accessed=10_000_000, transcendentals=0),
        name="galerkin_beside",
    )(sums, wt, y_left, y_right)

    sent = jax.ShapeDtypeStruct((W2, 5 * W2), bf16)
    own, to_a, to_b = pl.pallas_call(
        tail_kernel,
        in_specs=[vmem] * 6,
        out_specs=[vmem] * 3,
        out_shape=[own_shape, sent, sent],
        compiler_params=pltpu.CompilerParams(vmem_limit_bytes=TAIL_VMEM * MIB),
        cost_estimate=pl.CostEstimate(flops=600_000_000, bytes_accessed=8_000_000, transcendentals=0),
        name="galerkin_halo",
    )(own, up, dn, wt, halo_a, halo_b)

    from_a = lax.ppermute(to_a, "row", pairs_a)
    from_b = lax.ppermute(to_b, "row", pairs_b)

    return pl.pallas_call(
        final_kernel,
        in_specs=[vmem] * 3,
        out_specs=vmem,
        out_shape=own_shape,
        compiler_params=pltpu.CompilerParams(vmem_limit_bytes=8 * MIB),
        name="galerkin_sum",
    )(own, from_a, from_b)


def solution(mesh):
    return jax.shard_map(
        on_device,
        mesh=mesh,
        in_specs=(
            P("row", "col", None, None),
            P("row", "col", None),
            P("row", "col", None),
            P("row", "col", None),
            P("row", "col"),
            P("row", "col", None, None),
        ),
        out_specs=P("row", "col"),
        check_vma=False,
    )
```

```python
import functools

import jax
import jax.numpy as jnp
from jax import lax
from jax.experimental import pallas as pl
from jax.experimental.pallas import tpu as pltpu
from jax.sharding import PartitionSpec as P

B = 64
W2 = 128
SX, SY = 4, 64
FINE = SX * SY
HALF = SY // 2
TRASH_Z = 3 * FINE
N_WX = 128
N_W = N_WX + 32
TRASH_W = N_W
GROUP = 64
DEPTH = 4
FAR = 32
PT_STEPS = 1
UP_AT, DN_AT, SUMS = 3 * W2, 5 * W2, 7 * W2
SPARE_SUMS, SPARE_W = 144, 32
TAIL_VMEM = 24
MIB = 1024 * 1024
CHUNK = 128
f32, bf16 = jnp.float32, jnp.bfloat16


def swap_slots(x):
    return jnp.concatenate([x[..., B:], x[..., :B]], axis=-1)


def lanes_low(rows):
    return lax.broadcasted_iota(jnp.int32, (rows, W2), 1) < B


def place(axis):
    i = lax.axis_index(axis)
    return i == 0, i == lax.axis_size(axis) - 1, i % 2 == 0


def roll(x):
    return pltpu.roll(x, B, 1)


def add_two(ref, i, j, x, y):
    old_i, old_j = ref[i], ref[j]
    new_i = old_i + x
    ref[i] = new_i
    ref[j] = jnp.where(i == j, new_i, old_j) + y


def main_kernel(live_ref, ci_ref, zi_ref, hp_ref, a_hbm, p_hbm,
                sums_hbm, wt_hbm,
                a_v, p_v, pt_v, z_v, w_v, stage, stage_y, sums, list_s, sem_a, sem_p, sem_w):
    capacity = hp_ref.shape[0]
    live = live_ref[0, 0]
    first, last, _ = place("row")

    p_copies = [pltpu.make_async_copy(p_hbm.at[pl.ds(u * SY, SY)], p_v.at[pl.ds(u * SY, SY)], sem_p.at[u])
                for u in range(SX)]
    for c in p_copies:
        c.start()

    def a_copy(k):
        at = pl.ds(pl.multiple_of(k * (CHUNK * B), CHUNK * B), CHUNK * B)
        return pltpu.make_async_copy(a_hbm.at[:, at], a_v.at[:, at], sem_a.at[k])

    used_chunks = (live + CHUNK - 1) // CHUNK

    @pl.loop(0, used_chunks)
    def _(k):
        a_copy(k).start()

    @functools.partial(lax.fori_loop, 0, 32, init_val=jnp.int32(0))
    def count(k, count):
        z_v[pl.ds(k * 24, 24)] = jnp.zeros((24, B, W2), f32)
        w_v[pl.ds(k * 5, 5)] = jnp.zeros((5, W2, W2), f32)
        for s in range(capacity // 32):
            h = hp_ref[k * (capacity // 32) + s]
            list_s[count] = h
            count = count + 1 + (h >> 31)
        return count

    for u in range(SX):
        p_copies[u].wait()
        for half in range(2):
            q = u * 2 + half
            flag = {0: first, SX - 1: last}.get(u)

            @pl.loop(0, PT_STEPS)
            def _(k):
                for s in range(16 // PT_STEPS):
                    t = k * (16 // PT_STEPS) + s
                    at = pl.ds(q * HALF + t * 2, 2)
                    pair = p_v[at]
                    if half == 1:
                        pair = swap_slots(pair) if flag is None else jnp.where(flag, swap_slots(pair), pair)
                        p_v[at] = pair
                    pt_v[q * 16 + t] = pair.reshape(2 * B, W2).T

    for s in range(FAR):
        list_s[count + s] = jnp.int32(TRASH_W << 9)

    @pl.loop(0, used_chunks)
    def _(k):
        a_copy(k).wait()

    low = lanes_low(B)

    def far_dot(h):
        n = h >> 17
        par = (h >> 8) & 1
        r = h & 255
        a = a_v[:, pl.ds(pl.multiple_of((n >> 1) * W2, W2), W2)]
        a = jnp.where((n & 1) == par, a, swap_slots(a))
        a = jnp.where(low == (par == 0), a, jnp.zeros_like(a))
        even = (r & 1) == 0
        rhs = jnp.concatenate([jnp.where(even, a, jnp.zeros_like(a)),
                               jnp.where(even, jnp.zeros_like(a), a)], axis=0)
        return jnp.dot(pt_v[r >> 1], rhs, preferred_element_type=f32)

    @pl.loop(0, (count + FAR - 1) // FAR)
    def _(k):
        hs = [list_s[k * FAR + s] for s in range(FAR)]
        res = [far_dot(h) for h in hs]
        for s in range(0, FAR, 2):
            add_two(w_v, (hs[s] >> 9) & 255, (hs[s + 1] >> 9) & 255, res[s], res[s + 1])

    def w_copy(t):
        return pltpu.make_async_copy(
            stage.at[t], wt_hbm.at[t // 2, pl.ds((t % 2) * W2, W2)], sem_w.at[t])

    for t in range(4):
        @pl.loop(0, 32, unroll=8)
        def _(k):
            stage[t, :, pl.ds(pl.multiple_of(k * W2, W2), W2)] = w_v[t * 32 + k].astype(bf16)
        w_copy(t).start()

    @pl.loop(0, 32, unroll=8)
    def _(k):
        stage_y[:, pl.ds(pl.multiple_of(k * W2, W2), W2)] = w_v[N_WX + k].astype(bf16)

    y_copy = pltpu.make_async_copy(stage_y, wt_hbm.at[2, pl.ds(0, W2)], sem_w.at[4])
    y_copy.start()

    zero_p = jnp.zeros((B, W2), bf16)

    def near_dot(n):
        a = a_v[:, pl.ds(pl.multiple_of(n * B, W2), W2)]
        p0 = p_v[ci_ref[n]]
        p1 = p_v[ci_ref[n + 1]]
        w = jnp.concatenate([jnp.concatenate([p0, zero_p], axis=1),
                             jnp.concatenate([zero_p, p1], axis=1)], axis=0)
        return jnp.dot(a, w, preferred_element_type=f32)

    @pl.loop(0, (live + GROUP - 1) // GROUP)
    def _(g):
        n0 = g * GROUP
        res = {}
        for s in range(GROUP // 2 + DEPTH):
            if s < GROUP // 2:
                res[s] = near_dot(n0 + 2 * s)
            if s >= DEPTH:
                n, value = n0 + 2 * (s - DEPTH), res.pop(s - DEPTH)
                add_two(z_v, zi_ref[n], zi_ref[n + 1], value[:, :W2], value[:, W2:])

    low2 = lanes_low(W2)
    zb = jnp.zeros((B, W2), f32)
    for u in range(SX):
        mid = {0: first, SX - 1: last}.get(u)
        other = DN_AT if u == 0 else UP_AT
        for b in range(2):
            r0 = u * SY + b * HALF
            om = jnp.zeros((W2, W2), f32)
            oe = jnp.zeros((W2, 2 * W2), f32)
            for k in range(HALF // 4):
                r = r0 + 4 * k
                lhs = jnp.concatenate([pt_v[r // 2], pt_v[r // 2 + 1]], axis=1)
                zs = [z_v[pl.ds(g * FINE + r, 4)].reshape(4 * B, W2).astype(bf16) for g in range(3)]
                om += jnp.dot(lhs, zs[0], preferred_element_type=f32)
                oe += jnp.dot(lhs, jnp.concatenate(zs[1:], axis=1), preferred_element_type=f32)
            e0, e1 = oe[:, :W2], oe[:, W2:]
            same = om + jnp.where(low2, e0, roll(e1))
            adj = jnp.where(low2, roll(e0), e1)
            for g, c in ((1, same), (0 if u < 2 else 2, adj)):
                at = slice(g * W2, (g + 1) * W2)
                top, bot = c[:B], c[B:]
                if mid is not None:
                    slot = 0 if g == 1 else 1
                    sums[b * B:(b + 1) * B, other + slot * W2:other + (slot + 1) * W2] = jnp.where(mid, zb, bot)
                    bot = jnp.where(mid, bot, zb if b == 0 else top)
                    top = top if b == 0 else jnp.where(mid, top, zb)
                if b == 0 and (u == 0 or (u == 2 and g == 2)):
                    sums[:B, at] = top
                    sums[B:, at] = bot
                else:
                    sums[:B, at] += top
                    sums[B:, at] += bot

    out_copy = pltpu.make_async_copy(sums, sums_hbm.at[0], sem_w.at[5])
    out_copy.start()
    for t in range(4):
        w_copy(t).wait()
    y_copy.wait()
    out_copy.wait()


def beside_kernel(sums_hbm, wt_hbm, yl_ref, yr_ref,
                  own_ref, up_ref, dn_ref, wt_ref, sums, wy_ref, sem, sem_w):
    first, last, _ = place("row")
    no_l, no_r, _ = place("col")
    copies = [pltpu.make_async_copy(src, dst, sem.at[k]) for k, (src, dst) in enumerate(
        ((wt_hbm.at[2, pl.ds(0, W2)], wy_ref), (sums_hbm.at[0], sums)))]
    for c in copies:
        c.start()
    w_copies = [pltpu.make_async_copy(wt_hbm.at[t // 2, pl.ds((t % 2) * W2, W2)],
                                      wt_ref.at[t // 2, pl.ds((t % 2) * W2, W2)], sem_w.at[t]) for t in range(4)]
    for c in w_copies:
        c.start()

    low = lanes_low(W2)
    zl = jnp.zeros((B, W2), bf16)
    zt = jnp.zeros((W2, W2), f32)
    zb = jnp.zeros((B, W2), f32)
    rhs_y, is_mid = [], []
    for u in range(SX):
        mid = {0: first, SX - 1: last}.get(u)
        left = jnp.where(no_l, zl, yl_ref[u, 0])
        right = jnp.where(no_r, zl, yr_ref[u, 0])
        swapped = swap_slots(left)
        left = swapped if mid is None else jnp.where(mid, swapped, left)
        rhs_y.append(jnp.concatenate([jnp.concatenate([left, zl], axis=1),
                                      jnp.concatenate([zl, right], axis=1)], axis=0))
        is_mid.append(mid)
    for g in range(3):
        for k in (3 * g, 3 * g + 2):
            own_ref[:, k * W2:(k + 1) * W2] = zt

    copies[0].wait()
    for u in range(SX):
        mid = is_mid[u]
        other = dn_ref if u == 0 else up_ref
        for b in range(2):
            same = {-1: zt, 1: zt}
            adj = {-1: zt, 1: zt}
            for uc in range(max(0, u - 1), min(SX, u + 2)):
                k = uc * 8 + u * 2 + b
                ty = jnp.dot(wy_ref[:, k * W2:(k + 1) * W2], rhs_y[uc], preferred_element_type=f32)
                tl, tr = ty[:, :W2], ty[:, W2:]
                stays = is_mid[uc]
                if stays is None:
                    same[-1] += tl
                    same[1] += tr
                else:
                    same[-1] += jnp.where(stays, tl, jnp.where(low, zt, roll(tl)))
                    same[1] += jnp.where(stays, tr, jnp.where(low, tr, zt))
                    adj[-1] += jnp.where(stays, zt, jnp.where(low, zt, tl))
                    adj[1] += jnp.where(stays, zt, jnp.where(low, roll(tr), zt))
            adj_dx = 0 if u < 2 else 2
            for dy in (-1, 1):
                for dx, c in ((1, same[dy]), (adj_dx, adj[dy])):
                    at = slice((dx * 3 + dy + 1) * W2, (dx * 3 + dy + 2) * W2)
                    top, bot = c[:B], c[B:]
                    if mid is not None:
                        bot = jnp.where(mid, bot, zb if b == 0 else top)
                        top = top if b == 0 else jnp.where(mid, top, zb)
                    own_ref[:B, at] += top
                    own_ref[B:, at] += bot
            if mid is not None:
                q = slice(b * B, (b + 1) * B)
                for slot, c in ((2, same[-1]), (3, same[1]), (4, adj[-1] + adj[1])):
                    other[q, slot * W2:(slot + 1) * W2] = jnp.where(mid, zb, c[B:])

    copies[1].wait()
    for dx in range(3):
        own_ref[:, (3 * dx + 1) * W2:(3 * dx + 2) * W2] = sums[:, dx * W2:(dx + 1) * W2]
    up_ref[:, :2 * W2] = sums[:, UP_AT:DN_AT]
    dn_ref[:, :2 * W2] = sums[:, DN_AT:]
    for c in w_copies:
        c.wait()


def tail_kernel(own_in, up_in, dn_in, wt_ref, ha_ref, hb_ref, own_ref, oa_ref, ob_ref):
    first, last, even = place("row")
    low = lanes_low(2 * W2)
    middle = [own_in[:, (3 * dx + 1) * W2:(3 * dx + 2) * W2] for dx in range(3)]
    away = []
    for side, valid, src in ((0, jnp.logical_not(first), dn_in), (1, jnp.logical_not(last), up_in)):
        t = []
        for b in range(2):
            near = slice(b * HALF, (b + 1) * HALF)
            one, two = (ha_ref, hb_ref) if side == 1 else (hb_ref, ha_ref)
            rhs = jnp.where(even, one[near], two[near]).reshape(HALF * B, W2)
            lhs = wt_ref[side, :, b * HALF * B:(b + 1) * HALF * B]
            out = jnp.dot(lhs, rhs, preferred_element_type=f32)
            t.append(jnp.where(valid, out, jnp.zeros_like(out)))
        same = jnp.where(low, roll(t[0]), t[1])
        adj = jnp.where(low, t[0], roll(t[1]))
        dx = 0 if side == 0 else 2
        middle[1] = middle[1] + jnp.concatenate([same[:B], same[W2:W2 + B]], axis=0)
        middle[dx] = middle[dx] + jnp.concatenate([adj[:B], adj[W2:W2 + B]], axis=0)
        parts = [src[:, k * W2:(k + 1) * W2] for k in range(5)]
        for k, x in enumerate((same, adj)):
            parts[k] = parts[k] + jnp.concatenate([x[B:W2], x[W2 + B:]], axis=0)
        away.append(parts)
    for k in range(5):
        at = slice(k * W2, (k + 1) * W2)
        oa_ref[:, at] = jnp.where(even, away[1][k], away[0][k]).astype(bf16)
        ob_ref[:, at] = jnp.where(even, away[0][k], away[1][k]).astype(bf16)
    for dx in range(3):
        own_ref[:, (3 * dx + 1) * W2:(3 * dx + 2) * W2] = middle[dx]
        for dy in (0, 2):
            at = slice((3 * dx + dy) * W2, (3 * dx + dy + 1) * W2)
            own_ref[:, at] = own_in[:, at]


def edges_kernel(p_hbm, xa_ref, xb_ref, yr_ref, yl_ref, sem):
    _, _, even = place("row")
    to_a = jnp.where(even, SX - 1, 0)
    copies = [pltpu.make_async_copy(src, dst, sem.at[k]) for k, (src, dst) in enumerate((
        (p_hbm.at[to_a], xa_ref), (p_hbm.at[SX - 1 - to_a], xb_ref),
        (p_hbm.at[:, pl.ds(SY - 1, 1)], yr_ref), (p_hbm.at[:, pl.ds(0, 1)], yl_ref)))]
    for c in copies:
        c.start()
    for c in copies:
        c.wait()


def final_kernel(own_ref, ra_ref, rb_ref, out_ref):
    first, last, even = place("row")
    low = lanes_low(W2)
    zero = jnp.zeros((W2, W2), f32)
    a = [ra_ref[:, k * W2:(k + 1) * W2].astype(f32) for k in range(5)]
    b = [rb_ref[:, k * W2:(k + 1) * W2].astype(f32) for k in range(5)]
    lo = [jnp.where(first, zero, jnp.where(even, y, x)) for x, y in zip(a, b)]
    hi = [jnp.where(last, zero, jnp.where(even, x, y)) for x, y in zip(a, b)]
    sides = lo[4] + hi[4]
    extra = {
        0: lo[2], 1: lo[0], 2: lo[3],
        3: jnp.where(low, zero, sides), 4: lo[1] + hi[1], 5: jnp.where(low, sides, zero),
        6: hi[2], 7: hi[0], 8: hi[3],
    }
    for k, value in extra.items():
        out_ref[:, k * W2:(k + 1) * W2] = own_ref[:, k * W2:(k + 1) * W2] + value


def layout(rows, steps, cols, live, first, last):
    n = jnp.arange(rows.shape[0], dtype=jnp.int32)
    ur, br = rows // SY, (rows % SY) // HALF
    cx = ur + steps - 1
    outside = jnp.logical_or(cx < 0, cx >= SX)
    cy = jnp.where(outside, jnp.clip(cols - 1, 0, SY - 1), cols - 1)
    beside = jnp.logical_and(jnp.logical_not(outside), jnp.logical_or(cy < 0, cy >= SY))
    here = n < live
    far = jnp.logical_or(outside, beside)
    near = jnp.logical_and(here, jnp.logical_not(far))
    edge = jnp.logical_or(jnp.logical_and(cx == 0, first == 0), jnp.logical_and(cx == SX - 1, last == 0))
    kind = jnp.where(edge, 1 + cy // HALF, 0)
    ci = jnp.where(near, cx * SY + cy, 0)
    zi = jnp.where(near, kind * FINE + rows, TRASH_Z)
    side = (cx >= SX).astype(jnp.int32)
    y_side = (cy >= SY).astype(jnp.int32)
    wi = jnp.where(outside, (side * 2 + br) * HALF + cy // 2, N_WX + cx * 8 + ur * 2 + br)
    par = jnp.where(outside, cy % 2, y_side)
    hp = jnp.where(jnp.logical_and(here, far), (n << 17) | (wi << 9) | (par << 8) | rows, -1)
    return ci, zi, hp


def on_device(a_blocks, a_rows, a_steps, a_cols, a_live, p_blocks):
    capacity = a_rows.shape[2]
    n_row = lax.axis_size("row")
    i = lax.axis_index("row")

    def ring(x, axis, step):
        n = lax.axis_size(axis)
        return lax.ppermute(x, axis, [(k, (k + step) % n) for k in range(n)])

    pairs_a = [(k, min(k ^ 1, n_row - 1)) for k in range(n_row)]
    pairs_b = [(k, min(max(((k + 1) ^ 1) - 1, 0), n_row - 1)) for k in range(n_row)]

    smem = pl.BlockSpec(memory_space=pltpu.SMEM)
    vmem = pl.BlockSpec(memory_space=pltpu.VMEM)
    hbm = pl.BlockSpec(memory_space=pl.ANY)
    row = jax.ShapeDtypeStruct((SY, B, W2), bf16)
    column = jax.ShapeDtypeStruct((SX, 1, B, W2), bf16)
    x_a, x_b, p_right, p_left = pl.pallas_call(
        edges_kernel,
        in_specs=[hbm],
        out_specs=[vmem] * 4,
        out_shape=[row, row, column, column],
        scratch_shapes=[pltpu.SemaphoreType.DMA((4,))],
        compiler_params=pltpu.CompilerParams(vmem_limit_bytes=52 * MIB),
        name="edges",
    )(p_blocks)
    halo_a = lax.ppermute(x_a, "row", pairs_a)
    halo_b = lax.ppermute(x_b, "row", pairs_b)
    y_left = ring(p_right, "col", 1)
    y_right = ring(p_left, "col", -1)

    live = a_live.reshape(())
    first = (i == 0).astype(jnp.int32)
    last = (i == n_row - 1).astype(jnp.int32)
    ci, zi, hp = layout(a_rows.reshape(-1), a_steps.reshape(-1), a_cols.reshape(-1), live, first, last)

    sums, wt = pl.pallas_call(
        main_kernel,
        in_specs=[smem, smem, smem, smem, hbm, hbm],
        out_specs=[hbm, hbm],
        out_shape=[
            jax.ShapeDtypeStruct((SPARE_SUMS, W2, SUMS), f32),
            jax.ShapeDtypeStruct((SPARE_W, 2 * W2, SY * B), bf16),
        ],
        scratch_shapes=[
            pltpu.VMEM((B, capacity * B), bf16),
            pltpu.VMEM((FINE, B, W2), bf16),
            pltpu.VMEM((FINE // 2, W2, W2), bf16),
            pltpu.VMEM((TRASH_Z + 1, B, W2), f32),
            pltpu.VMEM((N_W + 1, W2, W2), f32),
            pltpu.VMEM((4, W2, SY * B), bf16),
            pltpu.VMEM((W2, 32 * W2), bf16),
            pltpu.VMEM((W2, SUMS), f32),
            pltpu.SMEM((capacity + FAR,), jnp.int32),
            pltpu.SemaphoreType.DMA((capacity // CHUNK,)),
            pltpu.SemaphoreType.DMA((SX,)),
            pltpu.SemaphoreType.DMA((6,)),
        ],
        compiler_params=pltpu.CompilerParams(vmem_limit_bytes=60 * MIB),
        cost_estimate=pl.CostEstimate(flops=4_000_000_000, bytes_accessed=20_000_000, transcendentals=0),
        name="galerkin_main",
    )(a_live, ci, zi, hp, a_blocks.reshape(B, capacity * B), p_blocks.reshape(FINE, B, W2))

    own_shape = jax.ShapeDtypeStruct((W2, 9 * W2), f32)
    own, up, dn, wt = pl.pallas_call(
        beside_kernel,
        in_specs=[hbm] * 2 + [vmem] * 2,
        out_specs=[vmem] * 4,
        out_shape=[
            own_shape,
            jax.ShapeDtypeStruct((W2, 5 * W2), f32),
            jax.ShapeDtypeStruct((W2, 5 * W2), f32),
            jax.ShapeDtypeStruct((2, 2 * W2, SY * B), bf16),
        ],
        scratch_shapes=[
            pltpu.VMEM((W2, SUMS), f32),
            pltpu.VMEM((W2, 32 * W2), bf16),
            pltpu.SemaphoreType.DMA((2,)),
            pltpu.SemaphoreType.DMA((4,)),
        ],
        compiler_params=pltpu.CompilerParams(vmem_limit_bytes=TAIL_VMEM * MIB),
        cost_estimate=pl.CostEstimate(flops=200_000_000, bytes_accessed=10_000_000, transcendentals=0),
        name="galerkin_beside",
    )(sums, wt, y_left, y_right)

    sent = jax.ShapeDtypeStruct((W2, 5 * W2), bf16)
    own, to_a, to_b = pl.pallas_call(
        tail_kernel,
        in_specs=[vmem] * 6,
        out_specs=[vmem] * 3,
        out_shape=[own_shape, sent, sent],
        compiler_params=pltpu.CompilerParams(vmem_limit_bytes=TAIL_VMEM * MIB),
        cost_estimate=pl.CostEstimate(flops=600_000_000, bytes_accessed=8_000_000, transcendentals=0),
        name="galerkin_halo",
    )(own, up, dn, wt, halo_a, halo_b)

    from_a = lax.ppermute(to_a, "row", pairs_a)
    from_b = lax.ppermute(to_b, "row", pairs_b)

    return pl.pallas_call(
        final_kernel,
        in_specs=[vmem] * 3,
        out_specs=vmem,
        out_shape=own_shape,
        compiler_params=pltpu.CompilerParams(vmem_limit_bytes=8 * MIB),
        name="galerkin_sum",
    )(own, from_a, from_b)


def solution(mesh):
    return jax.shard_map(
        on_device,
        mesh=mesh,
        in_specs=(
            P("row", "col", None, None),
            P("row", "col", None),
            P("row", "col", None),
            P("row", "col", None),
            P("row", "col"),
            P("row", "col", None, None),
        ),
        out_specs=P("row", "col"),
        check_vma=False,
    )
```

```python
import functools

import jax
import jax.numpy as jnp
from jax import lax
from jax.experimental import pallas as pl
from jax.experimental.pallas import tpu as pltpu
from jax.sharding import PartitionSpec as P

B = 64
W2 = 128
SX, SY = 4, 64
FINE = SX * SY
HALF = SY // 2
TRASH_Z = 3 * FINE
N_WX = 128
N_W = N_WX + 32
TRASH_W = N_W
GROUP = 128
DEPTH = 4
FAR = 32
PT_STEPS = 1
UP_AT, DN_AT, SUMS = 3 * W2, 5 * W2, 7 * W2
SPARE_SUMS, SPARE_W = 144, 32
TAIL_VMEM = 24
MIB = 1024 * 1024
CHUNK = 128
f32, bf16 = jnp.float32, jnp.bfloat16


def swap_slots(x):
    return jnp.concatenate([x[..., B:], x[..., :B]], axis=-1)


def lanes_low(rows):
    return lax.broadcasted_iota(jnp.int32, (rows, W2), 1) < B


def place(axis):
    i = lax.axis_index(axis)
    return i == 0, i == lax.axis_size(axis) - 1, i % 2 == 0


def roll(x):
    return pltpu.roll(x, B, 1)


def add_two(ref, i, j, x, y):
    old_i, old_j = ref[i], ref[j]
    new_i = old_i + x
    ref[i] = new_i
    ref[j] = jnp.where(i == j, new_i, old_j) + y


def main_kernel(live_ref, ci_ref, zi_ref, hp_ref, a_hbm, p_hbm,
                sums_hbm, wt_hbm,
                a_v, p_v, pt_v, z_v, w_v, stage, stage_y, sums, list_s, sem_a, sem_p, sem_w):
    capacity = hp_ref.shape[0]
    live = live_ref[0, 0]
    first, last, _ = place("row")

    p_copies = [pltpu.make_async_copy(p_hbm.at[pl.ds(u * SY, SY)], p_v.at[pl.ds(u * SY, SY)], sem_p.at[u])
                for u in range(SX)]
    for c in p_copies:
        c.start()

    def a_copy(k):
        at = pl.ds(pl.multiple_of(k * (CHUNK * B), CHUNK * B), CHUNK * B)
        return pltpu.make_async_copy(a_hbm.at[:, at], a_v.at[:, at], sem_a.at[k])

    used_chunks = (live + CHUNK - 1) // CHUNK

    @pl.loop(0, used_chunks)
    def _(k):
        a_copy(k).start()

    @functools.partial(lax.fori_loop, 0, 32, init_val=jnp.int32(0))
    def count(k, count):
        z_v[pl.ds(k * 24, 24)] = jnp.zeros((24, B, W2), f32)
        w_v[pl.ds(k * 5, 5)] = jnp.zeros((5, W2, W2), f32)
        for s in range(capacity // 32):
            h = hp_ref[k * (capacity // 32) + s]
            list_s[count] = h
            count = count + 1 + (h >> 31)
        return count

    for u in range(SX):
        p_copies[u].wait()
        for half in range(2):
            q = u * 2 + half
            flag = {0: first, SX - 1: last}.get(u)

            @pl.loop(0, PT_STEPS)
            def _(k):
                for s in range(16 // PT_STEPS):
                    t = k * (16 // PT_STEPS) + s
                    at = pl.ds(q * HALF + t * 2, 2)
                    pair = p_v[at]
                    if half == 1:
                        pair = swap_slots(pair) if flag is None else jnp.where(flag, swap_slots(pair), pair)
                        p_v[at] = pair
                    pt_v[q * 16 + t] = pair.reshape(2 * B, W2).T

    for s in range(FAR):
        list_s[count + s] = jnp.int32(TRASH_W << 9)

    @pl.loop(0, used_chunks)
    def _(k):
        a_copy(k).wait()

    low = lanes_low(B)

    def far_dot(h):
        n = h >> 17
        par = (h >> 8) & 1
        r = h & 255
        a = a_v[:, pl.ds(pl.multiple_of((n >> 1) * W2, W2), W2)]
        a = jnp.where((n & 1) == par, a, swap_slots(a))
        a = jnp.where(low == (par == 0), a, jnp.zeros_like(a))
        even = (r & 1) == 0
        rhs = jnp.concatenate([jnp.where(even, a, jnp.zeros_like(a)),
                               jnp.where(even, jnp.zeros_like(a), a)], axis=0)
        return jnp.dot(pt_v[r >> 1], rhs, preferred_element_type=f32)

    @pl.loop(0, (count + FAR - 1) // FAR)
    def _(k):
        hs = [list_s[k * FAR + s] for s in range(FAR)]
        res = [far_dot(h) for h in hs]
        for s in range(0, FAR, 2):
            add_two(w_v, (hs[s] >> 9) & 255, (hs[s + 1] >> 9) & 255, res[s], res[s + 1])

    def w_copy(t):
        return pltpu.make_async_copy(
            stage.at[t], wt_hbm.at[t // 2, pl.ds((t % 2) * W2, W2)], sem_w.at[t])

    for t in range(4):
        @pl.loop(0, 32, unroll=8)
        def _(k):
            stage[t, :, pl.ds(pl.multiple_of(k * W2, W2), W2)] = w_v[t * 32 + k].astype(bf16)
        w_copy(t).start()

    @pl.loop(0, 32, unroll=8)
    def _(k):
        stage_y[:, pl.ds(pl.multiple_of(k * W2, W2), W2)] = w_v[N_WX + k].astype(bf16)

    y_copy = pltpu.make_async_copy(stage_y, wt_hbm.at[2, pl.ds(0, W2)], sem_w.at[4])
    y_copy.start()

    zero_p = jnp.zeros((B, W2), bf16)

    def near_dot(n):
        a = a_v[:, pl.ds(pl.multiple_of(n * B, W2), W2)]
        p0 = p_v[ci_ref[n]]
        p1 = p_v[ci_ref[n + 1]]
        w = jnp.concatenate([jnp.concatenate([p0, zero_p], axis=1),
                             jnp.concatenate([zero_p, p1], axis=1)], axis=0)
        return jnp.dot(a, w, preferred_element_type=f32)

    @pl.loop(0, (live + GROUP - 1) // GROUP)
    def _(g):
        n0 = g * GROUP
        res = {}
        for s in range(GROUP // 2 + DEPTH):
            if s < GROUP // 2:
                res[s] = near_dot(n0 + 2 * s)
            if s >= DEPTH:
                n, value = n0 + 2 * (s - DEPTH), res.pop(s - DEPTH)
                add_two(z_v, zi_ref[n], zi_ref[n + 1], value[:, :W2], value[:, W2:])

    low2 = lanes_low(W2)
    zb = jnp.zeros((B, W2), f32)
    for u in range(SX):
        mid = {0: first, SX - 1: last}.get(u)
        other = DN_AT if u == 0 else UP_AT
        for b in range(2):
            r0 = u * SY + b * HALF
            om = jnp.zeros((W2, W2), f32)
            oe = jnp.zeros((W2, 2 * W2), f32)
            for k in range(HALF // 4):
                r = r0 + 4 * k
                lhs = jnp.concatenate([pt_v[r // 2], pt_v[r // 2 + 1]], axis=1)
                zs = [z_v[pl.ds(g * FINE + r, 4)].reshape(4 * B, W2).astype(bf16) for g in range(3)]
                om += jnp.dot(lhs, zs[0], preferred_element_type=f32)
                oe += jnp.dot(lhs, jnp.concatenate(zs[1:], axis=1), preferred_element_type=f32)
            e0, e1 = oe[:, :W2], oe[:, W2:]
            same = om + jnp.where(low2, e0, roll(e1))
            adj = jnp.where(low2, roll(e0), e1)
            for g, c in ((1, same), (0 if u < 2 else 2, adj)):
                at = slice(g * W2, (g + 1) * W2)
                top, bot = c[:B], c[B:]
                if mid is not None:
                    slot = 0 if g == 1 else 1
                    sums[b * B:(b + 1) * B, other + slot * W2:other + (slot + 1) * W2] = jnp.where(mid, zb, bot)
                    bot = jnp.where(mid, bot, zb if b == 0 else top)
                    top = top if b == 0 else jnp.where(mid, top, zb)
                if b == 0 and (u == 0 or (u == 2 and g == 2)):
                    sums[:B, at] = top
                    sums[B:, at] = bot
                else:
                    sums[:B, at] += top
                    sums[B:, at] += bot

    out_copy = pltpu.make_async_copy(sums, sums_hbm.at[0], sem_w.at[5])
    out_copy.start()
    for t in range(4):
        w_copy(t).wait()
    y_copy.wait()
    out_copy.wait()


def beside_kernel(sums_hbm, wt_hbm, yl_ref, yr_ref,
                  own_ref, up_ref, dn_ref, wt_ref, sums, wy_ref, sem, sem_w):
    first, last, _ = place("row")
    no_l, no_r, _ = place("col")
    copies = [pltpu.make_async_copy(src, dst, sem.at[k]) for k, (src, dst) in enumerate(
        ((wt_hbm.at[2, pl.ds(0, W2)], wy_ref), (sums_hbm.at[0], sums)))]
    for c in copies:
        c.start()
    w_copies = [pltpu.make_async_copy(wt_hbm.at[t // 2, pl.ds((t % 2) * W2, W2)],
                                      wt_ref.at[t // 2, pl.ds((t % 2) * W2, W2)], sem_w.at[t]) for t in range(4)]
    for c in w_copies:
        c.start()

    low = lanes_low(W2)
    zl = jnp.zeros((B, W2), bf16)
    zt = jnp.zeros((W2, W2), f32)
    zb = jnp.zeros((B, W2), f32)
    rhs_y, is_mid = [], []
    for u in range(SX):
        mid = {0: first, SX - 1: last}.get(u)
        left = jnp.where(no_l, zl, yl_ref[u, 0])
        right = jnp.where(no_r, zl, yr_ref[u, 0])
        swapped = swap_slots(left)
        left = swapped if mid is None else jnp.where(mid, swapped, left)
        rhs_y.append(jnp.concatenate([jnp.concatenate([left, zl], axis=1),
                                      jnp.concatenate([zl, right], axis=1)], axis=0))
        is_mid.append(mid)
    for g in range(3):
        for k in (3 * g, 3 * g + 2):
            own_ref[:, k * W2:(k + 1) * W2] = zt

    copies[0].wait()
    for u in range(SX):
        mid = is_mid[u]
        other = dn_ref if u == 0 else up_ref
        for b in range(2):
            same = {-1: zt, 1: zt}
            adj = {-1: zt, 1: zt}
            for uc in range(max(0, u - 1), min(SX, u + 2)):
                k = uc * 8 + u * 2 + b
                ty = jnp.dot(wy_ref[:, k * W2:(k + 1) * W2], rhs_y[uc], preferred_element_type=f32)
                tl, tr = ty[:, :W2], ty[:, W2:]
                stays = is_mid[uc]
                if stays is None:
                    same[-1] += tl
                    same[1] += tr
                else:
                    same[-1] += jnp.where(stays, tl, jnp.where(low, zt, roll(tl)))
                    same[1] += jnp.where(stays, tr, jnp.where(low, tr, zt))
                    adj[-1] += jnp.where(stays, zt, jnp.where(low, zt, tl))
                    adj[1] += jnp.where(stays, zt, jnp.where(low, roll(tr), zt))
            adj_dx = 0 if u < 2 else 2
            for dy in (-1, 1):
                for dx, c in ((1, same[dy]), (adj_dx, adj[dy])):
                    at = slice((dx * 3 + dy + 1) * W2, (dx * 3 + dy + 2) * W2)
                    top, bot = c[:B], c[B:]
                    if mid is not None:
                        bot = jnp.where(mid, bot, zb if b == 0 else top)
                        top = top if b == 0 else jnp.where(mid, top, zb)
                    own_ref[:B, at] += top
                    own_ref[B:, at] += bot
            if mid is not None:
                q = slice(b * B, (b + 1) * B)
                for slot, c in ((2, same[-1]), (3, same[1]), (4, adj[-1] + adj[1])):
                    other[q, slot * W2:(slot + 1) * W2] = jnp.where(mid, zb, c[B:])

    copies[1].wait()
    for dx in range(3):
        own_ref[:, (3 * dx + 1) * W2:(3 * dx + 2) * W2] = sums[:, dx * W2:(dx + 1) * W2]
    up_ref[:, :2 * W2] = sums[:, UP_AT:DN_AT]
    dn_ref[:, :2 * W2] = sums[:, DN_AT:]
    for c in w_copies:
        c.wait()


def tail_kernel(own_in, up_in, dn_in, wt_ref, ha_ref, hb_ref, own_ref, oa_ref, ob_ref):
    first, last, even = place("row")
    low = lanes_low(2 * W2)
    middle = [own_in[:, (3 * dx + 1) * W2:(3 * dx + 2) * W2] for dx in range(3)]
    away = []
    for side, valid, src in ((0, jnp.logical_not(first), dn_in), (1, jnp.logical_not(last), up_in)):
        t = []
        for b in range(2):
            near = slice(b * HALF, (b + 1) * HALF)
            one, two = (ha_ref, hb_ref) if side == 1 else (hb_ref, ha_ref)
            rhs = jnp.where(even, one[near], two[near]).reshape(HALF * B, W2)
            lhs = wt_ref[side, :, b * HALF * B:(b + 1) * HALF * B]
            out = jnp.dot(lhs, rhs, preferred_element_type=f32)
            t.append(jnp.where(valid, out, jnp.zeros_like(out)))
        same = jnp.where(low, roll(t[0]), t[1])
        adj = jnp.where(low, t[0], roll(t[1]))
        dx = 0 if side == 0 else 2
        middle[1] = middle[1] + jnp.concatenate([same[:B], same[W2:W2 + B]], axis=0)
        middle[dx] = middle[dx] + jnp.concatenate([adj[:B], adj[W2:W2 + B]], axis=0)
        parts = [src[:, k * W2:(k + 1) * W2] for k in range(5)]
        for k, x in enumerate((same, adj)):
            parts[k] = parts[k] + jnp.concatenate([x[B:W2], x[W2 + B:]], axis=0)
        away.append(parts)
    for k in range(5):
        at = slice(k * W2, (k + 1) * W2)
        oa_ref[:, at] = jnp.where(even, away[1][k], away[0][k]).astype(bf16)
        ob_ref[:, at] = jnp.where(even, away[0][k], away[1][k]).astype(bf16)
    for dx in range(3):
        own_ref[:, (3 * dx + 1) * W2:(3 * dx + 2) * W2] = middle[dx]
        for dy in (0, 2):
            at = slice((3 * dx + dy) * W2, (3 * dx + dy + 1) * W2)
            own_ref[:, at] = own_in[:, at]


def edges_kernel(p_hbm, xa_ref, xb_ref, yr_ref, yl_ref, sem):
    _, _, even = place("row")
    to_a = jnp.where(even, SX - 1, 0)
    copies = [pltpu.make_async_copy(src, dst, sem.at[k]) for k, (src, dst) in enumerate((
        (p_hbm.at[to_a], xa_ref), (p_hbm.at[SX - 1 - to_a], xb_ref),
        (p_hbm.at[:, pl.ds(SY - 1, 1)], yr_ref), (p_hbm.at[:, pl.ds(0, 1)], yl_ref)))]
    for c in copies:
        c.start()
    for c in copies:
        c.wait()


def final_kernel(own_ref, ra_ref, rb_ref, out_ref):
    first, last, even = place("row")
    low = lanes_low(W2)
    zero = jnp.zeros((W2, W2), f32)
    a = [ra_ref[:, k * W2:(k + 1) * W2].astype(f32) for k in range(5)]
    b = [rb_ref[:, k * W2:(k + 1) * W2].astype(f32) for k in range(5)]
    lo = [jnp.where(first, zero, jnp.where(even, y, x)) for x, y in zip(a, b)]
    hi = [jnp.where(last, zero, jnp.where(even, x, y)) for x, y in zip(a, b)]
    sides = lo[4] + hi[4]
    extra = {
        0: lo[2], 1: lo[0], 2: lo[3],
        3: jnp.where(low, zero, sides), 4: lo[1] + hi[1], 5: jnp.where(low, sides, zero),
        6: hi[2], 7: hi[0], 8: hi[3],
    }
    for k, value in extra.items():
        out_ref[:, k * W2:(k + 1) * W2] = own_ref[:, k * W2:(k + 1) * W2] + value


def layout(rows, steps, cols, live, first, last):
    n = jnp.arange(rows.shape[0], dtype=jnp.int32)
    ur, br = rows // SY, (rows % SY) // HALF
    cx = ur + steps - 1
    outside = jnp.logical_or(cx < 0, cx >= SX)
    cy = jnp.where(outside, jnp.clip(cols - 1, 0, SY - 1), cols - 1)
    beside = jnp.logical_and(jnp.logical_not(outside), jnp.logical_or(cy < 0, cy >= SY))
    here = n < live
    far = jnp.logical_or(outside, beside)
    near = jnp.logical_and(here, jnp.logical_not(far))
    edge = jnp.logical_or(jnp.logical_and(cx == 0, first == 0), jnp.logical_and(cx == SX - 1, last == 0))
    kind = jnp.where(edge, 1 + cy // HALF, 0)
    ci = jnp.where(near, cx * SY + cy, 0)
    zi = jnp.where(near, kind * FINE + rows, TRASH_Z)
    side = (cx >= SX).astype(jnp.int32)
    y_side = (cy >= SY).astype(jnp.int32)
    wi = jnp.where(outside, (side * 2 + br) * HALF + cy // 2, N_WX + cx * 8 + ur * 2 + br)
    par = jnp.where(outside, cy % 2, y_side)
    hp = jnp.where(jnp.logical_and(here, far), (n << 17) | (wi << 9) | (par << 8) | rows, -1)
    return ci, zi, hp


def on_device(a_blocks, a_rows, a_steps, a_cols, a_live, p_blocks):
    capacity = a_rows.shape[2]
    n_row = lax.axis_size("row")
    i = lax.axis_index("row")

    def ring(x, axis, step):
        n = lax.axis_size(axis)
        return lax.ppermute(x, axis, [(k, (k + step) % n) for k in range(n)])

    pairs_a = [(k, min(k ^ 1, n_row - 1)) for k in range(n_row)]
    pairs_b = [(k, min(max(((k + 1) ^ 1) - 1, 0), n_row - 1)) for k in range(n_row)]

    smem = pl.BlockSpec(memory_space=pltpu.SMEM)
    vmem = pl.BlockSpec(memory_space=pltpu.VMEM)
    hbm = pl.BlockSpec(memory_space=pl.ANY)
    row = jax.ShapeDtypeStruct((SY, B, W2), bf16)
    column = jax.ShapeDtypeStruct((SX, 1, B, W2), bf16)
    x_a, x_b, p_right, p_left = pl.pallas_call(
        edges_kernel,
        in_specs=[hbm],
        out_specs=[vmem] * 4,
        out_shape=[row, row, column, column],
        scratch_shapes=[pltpu.SemaphoreType.DMA((4,))],
        compiler_params=pltpu.CompilerParams(vmem_limit_bytes=52 * MIB),
        name="edges",
    )(p_blocks)
    halo_a = lax.ppermute(x_a, "row", pairs_a)
    halo_b = lax.ppermute(x_b, "row", pairs_b)
    y_left = ring(p_right, "col", 1)
    y_right = ring(p_left, "col", -1)

    live = a_live.reshape(())
    first = (i == 0).astype(jnp.int32)
    last = (i == n_row - 1).astype(jnp.int32)
    ci, zi, hp = layout(a_rows.reshape(-1), a_steps.reshape(-1), a_cols.reshape(-1), live, first, last)

    sums, wt = pl.pallas_call(
        main_kernel,
        in_specs=[smem, smem, smem, smem, hbm, hbm],
        out_specs=[hbm, hbm],
        out_shape=[
            jax.ShapeDtypeStruct((SPARE_SUMS, W2, SUMS), f32),
            jax.ShapeDtypeStruct((SPARE_W, 2 * W2, SY * B), bf16),
        ],
        scratch_shapes=[
            pltpu.VMEM((B, capacity * B), bf16),
            pltpu.VMEM((FINE, B, W2), bf16),
            pltpu.VMEM((FINE // 2, W2, W2), bf16),
            pltpu.VMEM((TRASH_Z + 1, B, W2), f32),
            pltpu.VMEM((N_W + 1, W2, W2), f32),
            pltpu.VMEM((4, W2, SY * B), bf16),
            pltpu.VMEM((W2, 32 * W2), bf16),
            pltpu.VMEM((W2, SUMS), f32),
            pltpu.SMEM((capacity + FAR,), jnp.int32),
            pltpu.SemaphoreType.DMA((capacity // CHUNK,)),
            pltpu.SemaphoreType.DMA((SX,)),
            pltpu.SemaphoreType.DMA((6,)),
        ],
        compiler_params=pltpu.CompilerParams(vmem_limit_bytes=60 * MIB),
        cost_estimate=pl.CostEstimate(flops=4_000_000_000, bytes_accessed=20_000_000, transcendentals=0),
        name="galerkin_main",
    )(a_live, ci, zi, hp, a_blocks.reshape(B, capacity * B), p_blocks.reshape(FINE, B, W2))

    own_shape = jax.ShapeDtypeStruct((W2, 9 * W2), f32)
    own, up, dn, wt = pl.pallas_call(
        beside_kernel,
        in_specs=[hbm] * 2 + [vmem] * 2,
        out_specs=[vmem] * 4,
        out_shape=[
            own_shape,
            jax.ShapeDtypeStruct((W2, 5 * W2), f32),
            jax.ShapeDtypeStruct((W2, 5 * W2), f32),
            jax.ShapeDtypeStruct((2, 2 * W2, SY * B), bf16),
        ],
        scratch_shapes=[
            pltpu.VMEM((W2, SUMS), f32),
            pltpu.VMEM((W2, 32 * W2), bf16),
            pltpu.SemaphoreType.DMA((2,)),
            pltpu.SemaphoreType.DMA((4,)),
        ],
        compiler_params=pltpu.CompilerParams(vmem_limit_bytes=TAIL_VMEM * MIB),
        cost_estimate=pl.CostEstimate(flops=200_000_000, bytes_accessed=10_000_000, transcendentals=0),
        name="galerkin_beside",
    )(sums, wt, y_left, y_right)

    sent = jax.ShapeDtypeStruct((W2, 5 * W2), bf16)
    own, to_a, to_b = pl.pallas_call(
        tail_kernel,
        in_specs=[vmem] * 6,
        out_specs=[vmem] * 3,
        out_shape=[own_shape, sent, sent],
        compiler_params=pltpu.CompilerParams(vmem_limit_bytes=TAIL_VMEM * MIB),
        cost_estimate=pl.CostEstimate(flops=600_000_000, bytes_accessed=8_000_000, transcendentals=0),
        name="galerkin_halo",
    )(own, up, dn, wt, halo_a, halo_b)

    from_a = lax.ppermute(to_a, "row", pairs_a)
    from_b = lax.ppermute(to_b, "row", pairs_b)

    return pl.pallas_call(
        final_kernel,
        in_specs=[vmem] * 3,
        out_specs=vmem,
        out_shape=own_shape,
        compiler_params=pltpu.CompilerParams(vmem_limit_bytes=8 * MIB),
        name="galerkin_sum",
    )(own, from_a, from_b)


def solution(mesh):
    return jax.shard_map(
        on_device,
        mesh=mesh,
        in_specs=(
            P("row", "col", None, None),
            P("row", "col", None),
            P("row", "col", None),
            P("row", "col", None),
            P("row", "col"),
            P("row", "col", None, None),
        ),
        out_specs=P("row", "col"),
        check_vma=False,
    )
```
